32 devices in a mesh: rep: 4 (over y, core), shard: 8 (over z, x).
Axes of the slice: x: 2, y: 2, z: 4, core: 2. Of those that a mesh axis runs over, the one named last changes fastest.
Arguments:
- tokens: bfloat16 [32768, 1024], P(('rep', 'shard')), may hold values from -6 to 6
- norm_gain_one: bfloat16 [1024], P('shard'), may hold values from 0.099609375 to 1.8984375
- in_weight: bfloat16 [1024, 3072], P('shard'), may hold values from -0.1875 to 0.1875
- conv_weight: bfloat16 [3, 1024], P(None, 'shard'), may hold values from -3.5 to 3.5
- out_weight: bfloat16 [1024, 1024], P(None, 'shard'), may hold values from -0.1875 to 0.1875
- norm_gain_two: bfloat16 [1024], P('shard'), may hold values from 0.099609375 to 1.8984375
- gate_weight: bfloat16 [1024, 4608], P('shard'), may hold values from -0.1875 to 0.1875
- up_weight: bfloat16 [1024, 4608], P('shard'), may hold values from -0.1875 to 0.1875
- down_weight: bfloat16 [4608, 1024], P(None, 'shard'), may hold values from -0.1875 to 0.1875
- cotangent: bfloat16 [32768, 1024], P(('rep', 'shard')), may hold values from -6 to 6
Outputs:
- block_out: bfloat16 [32768, 1024], P(('rep', 'shard'))
- tokens_grad: bfloat16 [32768, 1024], P(('rep', 'shard'))
- gain_one_grad: float32 [1024], P('shard')
- in_grad: float32 [1024, 3072], P('shard')
- conv_grad: float32 [3, 1024], P(None, 'shard')
- out_grad: float32 [1024, 1024], P(None, 'shard')
- gain_two_grad: float32 [1024], P('shard')
- gate_grad: float32 [1024, 4608], P('shard')
- up_grad: float32 [1024, 4608], P('shard')
- down_grad: float32 [4608, 1024], P(None, 'shard')
The draws below stay inside these ranges and needn't reach their ends.
All inputs are finite; a program needn't handle non-finite values.
Results may differ from the reference program's by a relative error of at most 0.018.
Values may be sent and summed in bfloat16 or wider, within the bound.
No kernel may reach another device: no remote copies, remote signals or barrier semaphores. Data moves between devices by JAX's collectives and lax.ppermute only.
A program may use at most 256 MiB of HBM per device.

```python
import jax
import jax.numpy as jnp
from jax import lax

D = 1024
FF = 4608
SEQ = 512
SEQS_DEV = 2
TOKENS = 32768


def spiked(entries, rng, source, target, shards_of, factor):
    owner, partner = [(jnp.arange(entries.shape[position]) // (entries.shape[position] // shards_of)).reshape([-1 if axis == position else 1 for axis in range(entries.ndim)]) for position in (source, target)]
    chosen = jax.random.permutation(rng, shards_of)[partner]
    strong = (owner == chosen) | (owner == (partner + shards_of // 2) % shards_of)
    return jnp.where(strong, factor * entries, entries)


def shard_levels(stream_key, extent, split, low, largest):
    gain = 1.0
    for axis_at, blocks in split:
        steps = jax.random.uniform(jax.random.fold_in(jax.random.fold_in(stream_key, 6), axis_at), (blocks,), jnp.float32, low / len(split), largest / len(split))
        gain = gain * jnp.repeat(jnp.exp(steps), extent[axis_at] // blocks).reshape((-1,) + (1,) * (len(extent) - 1 - axis_at))
    return gain


def scatter_about(own_key, shape, scale, bound, cuts=(), kind=jnp.bfloat16):
    entries = scale * jax.random.normal(own_key, shape, jnp.float32)
    if cuts:
        entries = entries * shard_levels(own_key, shape, cuts, -0.22, 0.18)
    return jnp.clip(entries, -bound, bound).astype(kind)


def bell_draw_with(rng, shape, deviation, reach, cuts, heavy, held_as=jnp.bfloat16):
    drawn = deviation * jax.random.normal(rng, shape, jnp.float32)
    if cuts:
        drawn = drawn * shard_levels(rng, shape, cuts, -0.22, 0.18)
    return jnp.clip(spiked(drawn, jax.random.fold_in(rng, 3), *heavy), -reach, reach).astype(held_as)


def setup_inputs(seed: int = 0) -> dict:
    splits = jax.random.split(jax.random.key(seed), 11)
    return {
        "tokens": scatter_about(splits[0], (TOKENS, D), 1.0, 6.0, ((0, 32),)),
        "norm_gain_one": jnp.clip(1.0 + 0.18 * jax.random.normal(splits[1], (D,), jnp.float32), 0.099609375, 1.8984375).astype(jnp.bfloat16),
        "in_weight": scatter_about(splits[2], (D, 3 * D), D ** -0.5, 0.1875, ((0, 8),)),
        "conv_weight": scatter_about(splits[3], (3, D), 3 ** -0.5, 3.5, ((1, 8),)),
        "out_weight": scatter_about(splits[4], (D, D), D ** -0.5, 0.1875, ((1, 8),)),
        "norm_gain_two": jnp.clip(1.0 + 0.18 * jax.random.normal(splits[5], (D,), jnp.float32), 0.099609375, 1.8984375).astype(jnp.bfloat16),
        "gate_weight": scatter_about(splits[6], (D, FF), D ** -0.5, 0.1875, ((0, 8),)),
        "up_weight": scatter_about(splits[7], (D, FF), D ** -0.5, 0.1875, ((0, 8),)),
        "down_weight": scatter_about(splits[8], (FF, D), (FF // 4) ** -0.5, 0.1875, ((1, 8),)),
        "cotangent": bell_draw_with(splits[9], (TOKENS, D), 1.0, 6.0, ((0, 32),), (0, 1, 32, 2.75)),
    }


EPSILON = 1e-05

@jax.custom_vjp
def low(v):
    return lax.optimization_barrier(v.astype(jnp.bfloat16)).astype(jnp.float32)

@jax.custom_vjp
def low_back(v):
    return v

def low_keep(v):
    return (low(v), None)

def low_pass(kept, grad):
    return (grad,)

def back_keep(v):
    return (v, None)

def back_low(kept, grad):
    return (low(grad),)
low.defvjp(low_keep, low_pass)
low_back.defvjp(back_keep, back_low)

def high_dot(left, right):
    return jnp.dot(left, right, precision=lax.Precision.HIGHEST)

def shift_back(values, steps):
    return jnp.pad(values[:, :values.shape[1] - steps], ((0, 0), (steps, 0), (0, 0)))

def forward(block_tokens, gain_one, weight_in, weight_conv, weight_out, gain_two, weight_gate, weight_up, weight_down):
    model_width = block_tokens.shape[1]
    inv_one = lax.rsqrt(lax.optimization_barrier(jnp.mean(block_tokens * block_tokens, -1, keepdims=True)) + EPSILON)
    normed_one = low(block_tokens * inv_one * gain_one)
    projected = low_back(high_dot(normed_one, weight_in))
    b_part = projected[:, :model_width]
    c_part = projected[:, model_width:2 * model_width]
    x_part = projected[:, 2 * model_width:]
    mixed_in = (b_part * x_part).reshape(-1, SEQ, model_width)
    conv_out = weight_conv[0] * shift_back(mixed_in, 2) + weight_conv[1] * shift_back(mixed_in, 1) + weight_conv[2] * mixed_in
    gated = low(c_part * conv_out.reshape(-1, model_width))
    branch = low_back(high_dot(gated, weight_out))
    middle = block_tokens + branch
    inv_two = lax.rsqrt(lax.optimization_barrier(jnp.mean(middle * middle, -1, keepdims=True)) + EPSILON)
    normed_two = low(middle * inv_two * gain_two)
    gate_pre = low_back(high_dot(normed_two, weight_gate))
    up_proj = low_back(high_dot(normed_two, weight_up))
    hidden = low(jax.nn.silu(gate_pre) * up_proj)
    return middle + high_dot(hidden, weight_down)

def reference(tokens, norm_gain_one, in_weight, conv_weight, out_weight, norm_gain_two, gate_weight, up_weight, down_weight, cotangent):
    params = tuple((p.astype(jnp.float32) for p in (norm_gain_one, in_weight, conv_weight, out_weight, norm_gain_two, gate_weight, up_weight, down_weight)))
    block_rows = SEQS_DEV * SEQ
    count_blocks = TOKENS // block_rows
    model_width = tokens.shape[1]
    inputs = tokens.astype(jnp.float32).reshape(count_blocks, block_rows, model_width)
    cot_blocks = cotangent.astype(jnp.float32).reshape(count_blocks, block_rows, model_width)

    def accumulate(totals, pair):
        block_in, block_cot = pair
        result, pullback = jax.vjp(forward, block_in, *params)
        grads = pullback(block_cot)
        new_totals = tuple((a + b for a, b in zip(totals, grads[1:])))
        return (new_totals, (result.astype(jnp.bfloat16), grads[0].astype(jnp.bfloat16)))
    start = tuple((jnp.zeros(p.shape, jnp.float32) for p in params))
    totals, (outputs, input_grads) = lax.scan(accumulate, start, (inputs, cot_blocks))
    block_out = outputs.reshape(TOKENS, model_width)
    tokens_grad = input_grads.reshape(TOKENS, model_width)
    return (block_out, tokens_grad, totals[0], totals[1], totals[2], totals[3], totals[4], totals[5], totals[6], totals[7])
```

```python
import functools

import jax
import jax.numpy as jnp
from jax import lax
from jax.sharding import PartitionSpec as P

SEQ = 512


EPSILON = 1e-05

AXES = ("rep", "shard")
PACK = 16


def plain_dot(left, right, kind=jnp.float32):
    return jnp.dot(left, right, preferred_element_type=jnp.float32).astype(kind)


def rows_dot(left, right):
    return lax.dot_general(
        left, right, (((1,), (1,)), ((), ())), preferred_element_type=jnp.float32
    )


def cols_dot(left, right):
    return lax.dot_general(
        left, right, (((0,), (0,)), ((), ())), preferred_element_type=jnp.float32
    ).astype(jnp.bfloat16)


def shift_back(values, steps):
    return jnp.pad(values[:, : values.shape[1] - steps], ((0, 0), (steps, 0), (0, 0)))


def shift_ahead(values, steps):
    return jnp.pad(values[:, steps:], ((0, 0), (0, steps), (0, 0)))


def norm_back(grad_norm, values, inv_rms, gain):
    scaled = grad_norm * gain
    grad_values = inv_rms * (
        scaled - values * inv_rms * inv_rms * jnp.mean(scaled * values, -1, keepdims=True)
    )
    grad_gain = jnp.sum(grad_norm * values * inv_rms, 0)
    return (grad_values, grad_gain)


def cycle_of(size):
    wide = size // 4
    walk = [(0, 0)]
    for row in range(4):
        cols = range(1, wide)
        walk += [(row, col) for col in (cols if row % 2 == 0 else reversed(cols))]
    walk += [(row, 0) for row in (3, 2, 1)]
    return [row * wide + col for row, col in walk]


def shards(
    reps,
    size,
    tokens,
    norm_gain_one,
    in_weight,
    conv_weight,
    out_weight,
    norm_gain_two,
    gate_weight,
    up_weight,
    down_weight,
    cotangent,
):
    bf16, f32 = jnp.bfloat16, jnp.float32
    width = tokens.shape[1]
    hidden_width = gate_weight.shape[1]
    block = width // size
    fq, dq = hidden_width // 4, width // 4
    ring = cycle_of(size)
    place = [ring.index(s) for s in range(size)]

    def pairs(move):
        return [
            (r * size + s, move(r, s)[0] * size + move(r, s)[1])
            for r in range(reps)
            for s in range(size)
        ]

    cw = pairs(lambda r, s: (r, ring[(place[s] + 1) % size]))
    ccw = pairs(lambda r, s: (r, ring[(place[s] - 1) % size]))
    to_core = pairs(lambda r, s: (r ^ 1, s))
    to_y = pairs(lambda r, s: (r ^ 2, s))

    def send(value, perm):
        return lax.ppermute(value, AXES, perm)

    rep = lax.axis_index("rep")
    core, ybit = rep % 2, (rep // 2) % 2
    at = jnp.asarray(place)[lax.axis_index("shard")]

    order = [0]
    for step in range(1, size // 2):
        order += [step, size - step]
    order += [size // 2]
    natural_block = jnp.asarray(ring)[(at - jnp.asarray(order)) % size]
    natural = (natural_block[:, None] * block + jnp.arange(block)[None, :]).reshape(-1)
    to_rel = (jnp.arange(width)[:, None] == natural[None, :]).astype(bf16)

    def quarter(i, j):
        return (core ^ i) * 2 + (ybit ^ j)

    quarters = ((0, 0), (0, 1), (1, 0), (1, 1))
    natural_feature = (
        jnp.stack([quarter(i, j) for i, j in quarters])[:, None] * dq + jnp.arange(dq)[None, :]
    ).reshape(-1)

    def ring_gather(piece, flip):
        got = {0: piece}
        n_cw = size // 2 - (1 if flip else 0)
        up = down = piece
        for step in range(1, size // 2 + 1):
            if step <= n_cw:
                up = got[step] = send(up, cw)
            if step <= size - 1 - n_cw:
                down = got[size - step] = send(down, ccw)
        return got

    def paired(got):
        return [[got[s], got[size - s]] for s in range(1, size // 2)] + [[got[size // 2]]]

    def ring_scatter(blocks, flip):
        n_cw = size // 2 - (1 if flip else 0)
        n_ccw = size - 1 - n_cw
        up = down = None
        for step in range(size // 2, 0, -1):
            if step <= n_cw:
                own = blocks[size - step]
                up = send(own if up is None else up + own, cw)
            if step <= n_ccw:
                own = blocks[step]
                down = send(own if down is None else down + own, ccw)
        return (blocks[0].astype(f32) + up.astype(f32) + down.astype(f32)).astype(bf16)

    def add(left, right):
        return (left.astype(f32) + right.astype(f32)).astype(bf16)

    def high_reps(value):
        step = 4
        while step < reps:
            value = add(value, send(value, pairs(lambda r, s: (r ^ step, s))))
            step *= 2
        return value

    def part(value, axis, i, j, extent):
        return lax.dynamic_slice_in_dim(value, quarter(i, j) * extent, extent, axis)

    def in_part(i, j):
        return part(in_weight.reshape(block, 3, width), 2, i, j, dq).reshape(block, 3 * dq)

    def gu_part(i, j):
        return jnp.concatenate(
            [part(gate_weight, 1, i, j, fq), part(up_weight, 1, i, j, fq)], 1
        )

    small = jnp.concatenate([norm_gain_one, norm_gain_two, conv_weight.reshape(-1)])
    pack = jnp.pad(small[None, :], ((0, PACK - 1), (0, 3 * dq - small.shape[0])))

    in_got = ring_gather(jnp.concatenate([in_part(0, 0), pack], 0), False)
    gu_got = ring_gather(gu_part(0, 0), True)
    out_own = jnp.concatenate([part(out_weight, 0, 0, 0, dq), part(out_weight, 0, 0, 1, dq)], 0)
    out_got = ring_gather(out_own, True)
    down_own = jnp.concatenate([part(down_weight, 0, 0, 0, fq), part(down_weight, 0, 0, 1, fq)], 0)
    down_got = ring_gather(down_own, False)

    def quarters_of(got, mine):
        groups = [jnp.concatenate(g, 0) for g in paired(got)]
        q00 = jnp.concatenate([got[0]] + groups, 0)
        q01 = jnp.concatenate([mine] + [send(g, to_y) for g in groups], 0)
        return q00, q01, send(q00, to_core), send(q01, to_core)

    in_rows = {b: v[:block] for b, v in in_got.items()}
    packs = jnp.stack([in_got[b][block, : 5 * block] for b in order], 0).reshape(size, 5, block)
    in_q = quarters_of(in_rows, in_part(0, 1))
    gu_q = quarters_of(gu_got, gu_part(0, 1))
    out_half = jnp.concatenate([out_got[b] for b in order], 1)
    out_full = jnp.concatenate([out_half, send(out_half, to_core)], 0)
    down_half = jnp.concatenate([down_got[b] for b in order], 1)
    down_h = (down_half, send(down_half, to_core))

    gain_one_f = packs[:, 0].reshape(-1).astype(f32)
    gain_two_f = packs[:, 1].reshape(-1).astype(f32)
    to_feature = (natural[:, None] == natural_feature[None, :]).astype(bf16)
    taps = plain_dot(packs[:, 2:].transpose(1, 0, 2).reshape(3, width), to_feature)

    tokens_f = plain_dot(tokens, to_rel)
    cot = plain_dot(cotangent, to_rel, bf16)
    inv_one = lax.rsqrt(jnp.mean(tokens_f * tokens_f, -1, keepdims=True) + EPSILON)
    normed_one = (tokens_f * inv_one * gain_one_f).astype(bf16)
    projected = [plain_dot(normed_one, w) for w in in_q]
    b_part = jnp.concatenate([p[:, :dq] for p in projected], 1)
    c_part = jnp.concatenate([p[:, dq : 2 * dq] for p in projected], 1)
    x_part = jnp.concatenate([p[:, 2 * dq :] for p in projected], 1)
    mixed_in = (b_part * x_part).reshape(-1, SEQ, width)
    conv_out = (
        taps[0] * shift_back(mixed_in, 2) + taps[1] * shift_back(mixed_in, 1) + taps[2] * mixed_in
    ).reshape(-1, width)
    gated = (c_part * conv_out).astype(bf16)
    middle = tokens_f + plain_dot(gated, out_full)
    inv_two = lax.rsqrt(jnp.mean(middle * middle, -1, keepdims=True) + EPSILON)
    normed_two = (middle * inv_two * gain_two_f).astype(bf16)
    pre = [plain_dot(normed_two, w) for w in gu_q]
    gate_pre = [p[:, :fq] for p in pre]
    up_proj = [p[:, fq:] for p in pre]
    sigma = [jax.nn.sigmoid(g) for g in gate_pre]
    silu = [g * s for g, s in zip(gate_pre, sigma)]
    hidden = [(s * u).astype(bf16) for s, u in zip(silu, up_proj)]
    hidden_h = [jnp.concatenate(hidden[2 * i : 2 * i + 2], 1) for i in range(2)]
    block_out = (
        middle + plain_dot(hidden_h[0], down_h[0]) + plain_dot(hidden_h[1], down_h[1])
    ).astype(bf16)

    def cut(value, axis, at_block, count=1):
        start = at_block * block
        return lax.slice_in_dim(value, start, start + count * block, axis=axis)

    def blocks_of(value, axis):
        return {b: cut(value, axis, n) for n, b in enumerate(order)}

    down_local = [cols_dot(h, cot) for h in hidden_h]
    down_sum = add(down_local[0], send(down_local[1], to_core))
    down_slice = ring_scatter(blocks_of(down_sum, 1), True)

    cot_f = cot.astype(f32)
    hidden_grad_h = [rows_dot(cot, w) for w in down_h]
    hidden_grad = [h[:, j * fq : (j + 1) * fq] for h in hidden_grad_h for j in range(2)]
    gu_back = [
        jnp.concatenate(
            [
                (hg * u * s * (1.0 + g * (1.0 - s))).astype(bf16),
                (hg * sl).astype(bf16),
            ],
            1,
        )
        for hg, u, s, g, sl in zip(hidden_grad, up_proj, sigma, gate_pre, silu)
    ]
    gu_local = [cols_dot(normed_two, b) for b in gu_back]
    gu_sum = [add(gu_local[j], send(gu_local[2 + j], to_core)) for j in range(2)]
    cuts = [(size - 3, 3), (3, size - 6), (0, 3)]
    gu_rows = {}
    for start, count in cuts:
        away = send(cut(gu_sum[1], 0, start, count), to_y)
        both = add(cut(gu_sum[0], 0, start, count), away)
        for n in range(count):
            gu_rows[order[start + n]] = cut(both, 0, n)

    normed_two_grad = sum(rows_dot(b, w) for b, w in zip(gu_back, gu_q))
    middle_norm_grad, gain_two_local = norm_back(normed_two_grad, middle, inv_two, gain_two_f)
    middle_grad = cot_f + middle_norm_grad
    branch_back = middle_grad.astype(bf16)
    out_local = cols_dot(gated, branch_back)
    half = out_local.shape[0] // 2
    out_sum = add(out_local[:half], send(out_local[half:], to_core))
    out_slice = ring_scatter(blocks_of(out_sum, 1), True)
    gated_grad = rows_dot(branch_back, out_full)
    c_grad = gated_grad * conv_out
    conv_grad_in = (gated_grad * c_part).reshape(-1, SEQ, width)
    conv_local = jnp.stack(
        [
            jnp.sum(conv_grad_in * shift_back(mixed_in, 2), (0, 1)),
            jnp.sum(conv_grad_in * shift_back(mixed_in, 1), (0, 1)),
            jnp.sum(conv_grad_in * mixed_in, (0, 1)),
        ],
        0,
    )
    mixed_grad = (
        taps[2] * conv_grad_in
        + taps[1] * shift_ahead(conv_grad_in, 1)
        + taps[0] * shift_ahead(conv_grad_in, 2)
    ).reshape(-1, width)
    b_back = (mixed_grad * x_part).astype(bf16)
    c_back = c_grad.astype(bf16)
    x_back = (mixed_grad * b_part).astype(bf16)

    def of_quarter(value, n):
        return value[:, n * dq : (n + 1) * dq]

    projected_back = [
        jnp.concatenate([of_quarter(v, n) for v in (b_back, c_back, x_back)], 1) for n in range(4)
    ]
    in_back_h = [jnp.concatenate(projected_back[2 * i : 2 * i + 2], 1) for i in range(2)]
    in_local = [cols_dot(normed_one, b) for b in in_back_h]
    normed_one_grad = sum(rows_dot(b, w) for b, w in zip(projected_back, in_q))
    tokens_norm_grad, gain_one_local = norm_back(normed_one_grad, tokens_f, inv_one, gain_one_f)
    tokens_grad = (middle_grad + tokens_norm_grad).astype(bf16)

    conv_rel = lax.dot_general(
        conv_local.astype(bf16), to_feature, (((1,), (1,)), ((), ())), preferred_element_type=f32
    ).astype(bf16)
    small_grad = jnp.concatenate(
        [gain_one_local.astype(bf16)[None], gain_two_local.astype(bf16)[None], conv_rel], 0
    )
    small_rows = small_grad.reshape(5, size, block).transpose(1, 0, 2).reshape(size, 5 * block)
    small_rows = jnp.pad(small_rows, ((0, 0), (0, 6 * dq - 5 * block)))
    small_sum = jnp.pad(small_rows[:, None], ((0, 0), (0, PACK - 1), (0, 0)))

    def with_small(value):
        rows = value.reshape(size, block, 6 * dq)
        return jnp.concatenate([rows, small_sum], 1)

    in_mine = with_small(in_local[0])
    in_sum = add(in_mine, send(with_small(in_local[1]), to_core))
    in_slice = ring_scatter({b: in_sum[n] for n, b in enumerate(order)}, False)
    gu_slice = ring_scatter(gu_rows, False)

    def over_y(value):
        return high_reps(add(value, send(value, to_y)))

    def swap(flag, first, second, axis):
        return jnp.where(
            flag == 0,
            jnp.concatenate([first, second], axis),
            jnp.concatenate([second, first], axis),
        )

    def y_ordered(value, axis):
        n = value.shape[axis] // 2
        return swap(
            ybit,
            lax.slice_in_dim(value, 0, n, axis=axis),
            lax.slice_in_dim(value, n, 2 * n, axis=axis),
            axis,
        )

    def whole(value):
        total = over_y(y_ordered(value, 0))
        return swap(core, total, send(total, to_core), 0).astype(f32)

    down_grad = whole(down_slice)
    out_grad = whole(out_slice)
    in_total = over_y(
        jnp.concatenate([y_ordered(in_slice[:block], 1), in_slice[block:]], 0)
    )
    in_mine_total = in_total[:block].reshape(block, 2, 3, dq)
    in_other_total = send(in_total[:block], to_core).reshape(block, 2, 3, dq)
    in_grad = (
        swap(core, in_mine_total, in_other_total, 1)
        .transpose(0, 2, 1, 3)
        .reshape(block, 3 * width)
        .astype(f32)
    )
    small_total = in_total[block, : 5 * block].astype(f32).reshape(5, block)
    gu_total = high_reps(gu_slice)
    gu_other = send(gu_total, to_y)
    gu_both = jnp.stack([gu_total, gu_other], 0)
    gu_far = send(gu_both, to_core)

    def gu_out(start):
        own = swap(ybit, gu_both[0][:, start : start + fq], gu_both[1][:, start : start + fq], 1)
        far = swap(ybit, gu_far[0][:, start : start + fq], gu_far[1][:, start : start + fq], 1)
        return swap(core, own, far, 1).astype(f32)

    gate_grad, up_grad = gu_out(0), gu_out(fq)

    def to_natural(value):
        return rows_dot(value, to_rel).astype(bf16)

    return (
        to_natural(block_out),
        to_natural(tokens_grad),
        small_total[0],
        in_grad,
        small_total[2:],
        out_grad,
        small_total[1],
        gate_grad,
        up_grad,
        down_grad,
    )


def solution(mesh):
    in_specs = (
        P(("rep", "shard"), None),
        P("shard"),
        P("shard", None),
        P(None, "shard"),
        P(None, "shard"),
        P("shard"),
        P("shard", None),
        P("shard", None),
        P(None, "shard"),
        P(("rep", "shard"), None),
    )
    out_specs = (
        P(("rep", "shard"), None),
        P(("rep", "shard"), None),
        P("shard"),
        P("shard", None),
        P(None, "shard"),
        P(None, "shard"),
        P("shard"),
        P("shard", None),
        P("shard", None),
        P(None, "shard"),
    )
    body = functools.partial(shards, mesh.shape["rep"], mesh.shape["shard"])
    return jax.shard_map(body, mesh=mesh, in_specs=in_specs, out_specs=out_specs, check_vma=False)
```

```python
import functools

import jax
import jax.numpy as jnp
from jax import lax
from jax.sharding import PartitionSpec as P

SEQ = 512


EPSILON = 1e-05

AXES = ("rep", "shard")
PACK = 16


def plain_dot(left, right, kind=jnp.float32):
    return jnp.dot(left, right, preferred_element_type=jnp.float32).astype(kind)


def rows_dot(left, right):
    return lax.dot_general(
        left, right, (((1,), (1,)), ((), ())), preferred_element_type=jnp.float32
    )


def cols_dot(left, right):
    return lax.dot_general(
        left, right, (((0,), (0,)), ((), ())), preferred_element_type=jnp.float32
    ).astype(jnp.bfloat16)


def shift_back(values, steps):
    return jnp.pad(values[:, : values.shape[1] - steps], ((0, 0), (steps, 0), (0, 0)))


def shift_ahead(values, steps):
    return jnp.pad(values[:, steps:], ((0, 0), (0, steps), (0, 0)))


def norm_back(grad_norm, values, inv_rms, gain):
    scaled = grad_norm * gain
    grad_values = inv_rms * (
        scaled - values * inv_rms * inv_rms * jnp.mean(scaled * values, -1, keepdims=True)
    )
    grad_gain = jnp.sum(grad_norm * values * inv_rms, 0)
    return (grad_values, grad_gain)


def cycle_of(size):
    wide = size // 4
    walk = [(0, 0)]
    for row in range(4):
        cols = range(1, wide)
        walk += [(row, col) for col in (cols if row % 2 == 0 else reversed(cols))]
    walk += [(row, 0) for row in (3, 2, 1)]
    return [row * wide + col for row, col in walk]


def shards(
    reps,
    size,
    tokens,
    norm_gain_one,
    in_weight,
    conv_weight,
    out_weight,
    norm_gain_two,
    gate_weight,
    up_weight,
    down_weight,
    cotangent,
):
    bf16, f32 = jnp.bfloat16, jnp.float32
    width = tokens.shape[1]
    hidden_width = gate_weight.shape[1]
    block = width // size
    fq, dq = hidden_width // 4, width // 4
    ring = cycle_of(size)
    place = [ring.index(s) for s in range(size)]

    def pairs(move):
        return [
            (r * size + s, move(r, s)[0] * size + move(r, s)[1])
            for r in range(reps)
            for s in range(size)
        ]

    cw = pairs(lambda r, s: (r, ring[(place[s] + 1) % size]))
    ccw = pairs(lambda r, s: (r, ring[(place[s] - 1) % size]))
    to_core = pairs(lambda r, s: (r ^ 1, s))
    to_y = pairs(lambda r, s: (r ^ 2, s))

    def send(value, perm):
        return lax.ppermute(value, AXES, perm)

    rep = lax.axis_index("rep")
    core, ybit = rep % 2, (rep // 2) % 2
    at = jnp.asarray(place)[lax.axis_index("shard")]

    order = [0]
    for step in range(1, size // 2):
        order += [step, size - step]
    order += [size // 2]
    natural_block = jnp.asarray(ring)[(at - jnp.asarray(order)) % size]
    natural = (natural_block[:, None] * block + jnp.arange(block)[None, :]).reshape(-1)
    to_rel = (jnp.arange(width)[:, None] == natural[None, :]).astype(bf16)

    def quarter(i, j):
        return (core ^ i) * 2 + (ybit ^ j)

    quarters = ((0, 0), (0, 1), (1, 0), (1, 1))
    natural_feature = (
        jnp.stack([quarter(i, j) for i, j in quarters])[:, None] * dq + jnp.arange(dq)[None, :]
    ).reshape(-1)

    last = []

    def ordered_round(sends, work=None, args=()):
        leaves, tree = jax.tree.flatten(([v for v, _ in sends], tuple(args)))
        held = lax.optimization_barrier(tuple(leaves) + tuple(last))
        values, args = jax.tree.unflatten(tree, held[: len(leaves)])
        got = [send(v, perm) for v, (_, perm) in zip(values, sends)]
        made = work(*args) if work is not None else None
        last[:] = got + jax.tree.leaves(made)
        return got, made

    class Gather:
        def __init__(self, piece, flip):
            self.got = {0: piece}
            self.n_cw = size // 2 - (1 if flip else 0)
            self.n_ccw = size - 1 - self.n_cw
            self.step = 0

        def sends(self):
            self.step += 1
            self.to = []
            out = []
            if self.step <= self.n_cw:
                out.append((self.got[self.step - 1], cw))
                self.to.append(self.step)
            if self.step <= self.n_ccw:
                out.append((self.got[(size - self.step + 1) % size], ccw))
                self.to.append(size - self.step)
            return out

        def take(self, got):
            for b in self.to:
                self.got[b] = got.pop(0)

        def done(self):
            return self.step == size // 2

        def rows(self):
            return jnp.concatenate([self.got[b] for b in order], 0)

        def cols(self):
            return jnp.concatenate([self.got[b] for b in order], 1)

    class Scatter:
        def __init__(self, own, flip):
            self.own = own
            self.n_cw = size // 2 - (1 if flip else 0)
            self.n_ccw = size - 1 - self.n_cw
            self.step = size // 2 + 1
            self.up = self.down = None

        def sends(self):
            self.step -= 1
            out = []
            if self.step <= self.n_cw:
                out.append((total(*self.own(size - self.step), self.up), cw))
            if self.step <= self.n_ccw:
                out.append((total(*self.own(self.step), self.down), ccw))
            return out

        def take(self, got):
            if self.step <= self.n_cw:
                self.up = got.pop(0)
            if self.step <= self.n_ccw:
                self.down = got.pop(0)

        def done(self):
            return self.step == 1

        def result(self):
            return total(*self.own(0), self.up, self.down)

    def total(*values):
        values = [v for v in values if v is not None]
        if len(values) == 1:
            return values[0]
        return sum(v.astype(f32) for v in values).astype(bf16)

    def add(left, right):
        return total(left, right)

    def both_rounds(rings, others=(), work=None, args=()):
        sends = []
        counts = []
        for r in rings:
            mine = r.sends()
            counts.append(len(mine))
            sends += mine
        got, made = ordered_round(sends + list(others), work, args)
        for r, n in zip(rings, counts):
            r.take(got[:n])
            got = got[n:]
        return got, made

    def finish(*rings):
        while rings := [r for r in rings if not r.done()]:
            both_rounds(rings)

    def high_reps(value):
        step = 4
        while step < reps:
            value = add(value, send(value, pairs(lambda r, s: (r ^ step, s))))
            step *= 2
        return value

    def part(value, axis, i, j, extent):
        return lax.dynamic_slice_in_dim(value, quarter(i, j) * extent, extent, axis)

    def in_part(i, j):
        return part(in_weight.reshape(block, 3, width), 2, i, j, dq).reshape(block, 3 * dq)

    def gu_part(i, j):
        return jnp.concatenate(
            [part(gate_weight, 1, i, j, fq), part(up_weight, 1, i, j, fq)], 1
        )

    def half_part(value, extent):
        return jnp.concatenate([part(value, 0, 0, j, extent) for j in range(2)], 0)

    small = jnp.concatenate([norm_gain_one, norm_gain_two, conv_weight.reshape(-1)])
    pack = jnp.pad(small[None, :], ((0, PACK - 1), (0, 6 * dq - small.shape[0])))
    in_ring = Gather(
        jnp.concatenate([jnp.concatenate([in_part(0, 0), in_part(0, 1)], 1), pack], 0), False
    )
    out_ring = Gather(half_part(out_weight, dq), True)
    gu_ring = Gather(gu_part(0, 0), True)
    down_ring = Gather(half_part(down_weight, fq), False)
    far_pieces = {0: gu_part(0, 1)}
    far_order = [b for b in order if b != 0]

    def far_send():
        b = far_order[len(far_pieces) - 1]
        return (gu_ring.got[b], to_y)

    def far_take(value):
        far_pieces[far_order[len(far_pieces) - 1]] = value

    def prepare(tokens, cotangent):
        tokens_f = plain_dot(tokens, to_rel)
        inv_one = lax.rsqrt(jnp.mean(tokens_f * tokens_f, -1, keepdims=True) + EPSILON)
        return tokens_f, plain_dot(cotangent, to_rel, bf16), inv_one

    _, (tokens_f, cot, inv_one) = both_rounds([in_ring], (), prepare, (tokens, cotangent))
    both_rounds([in_ring, out_ring])
    both_rounds([in_ring, out_ring])
    both_rounds([in_ring, out_ring])
    finish(in_ring)
    in_half = jnp.concatenate([in_ring.got[b][:block] for b in order], 0)
    packs = jnp.stack([in_ring.got[b][block, : 5 * block] for b in order], 0).reshape(
        size, 5, block
    )
    gain_one_f = packs[:, 0].reshape(-1).astype(f32)
    gain_two_f = packs[:, 1].reshape(-1).astype(f32)
    to_feature = (natural[:, None] == natural_feature[None, :]).astype(bf16)
    taps = plain_dot(packs[:, 2:].transpose(1, 0, 2).reshape(3, width), to_feature)

    def project_first(tokens_f, inv_one, gain, weight):
        normed_one = (tokens_f * inv_one * gain).astype(bf16)
        return normed_one, plain_dot(normed_one, weight)

    (in_far,), (normed_one, projected_0) = both_rounds(
        [gu_ring, out_ring],
        [(in_half, to_core)],
        project_first,
        (tokens_f, inv_one, gain_one_f, in_half),
    )
    in_h = (in_half, in_far)
    finish(out_ring)
    out_half = out_ring.cols()
    (far, out_far), projected_1 = both_rounds(
        [gu_ring], [far_send(), (out_half, to_core)], plain_dot, (normed_one, in_far)
    )
    far_take(far)
    out_full = jnp.concatenate([out_half, out_far], 0)

    def convolve(p0, p1):
        projected = [p[:, 3 * dq * j : 3 * dq * (j + 1)] for p in (p0, p1) for j in range(2)]
        b_part = jnp.concatenate([p[:, :dq] for p in projected], 1)
        c_part = jnp.concatenate([p[:, dq : 2 * dq] for p in projected], 1)
        x_part = jnp.concatenate([p[:, 2 * dq :] for p in projected], 1)
        mixed_in = (b_part * x_part).reshape(-1, SEQ, width)
        conv_out = (
            taps[0] * shift_back(mixed_in, 2)
            + taps[1] * shift_back(mixed_in, 1)
            + taps[2] * mixed_in
        ).reshape(-1, width)
        gated = (c_part * conv_out).astype(bf16)
        return b_part, c_part, x_part, mixed_in, conv_out, gated

    (far,), (b_part, c_part, x_part, mixed_in, conv_out, gated) = both_rounds(
        [gu_ring], [far_send()], convolve, (projected_0, projected_1)
    )
    far_take(far)

    def mid(tokens_f, gated, weight):
        middle = tokens_f + plain_dot(gated, weight)
        inv_two = lax.rsqrt(jnp.mean(middle * middle, -1, keepdims=True) + EPSILON)
        return middle, inv_two, (middle * inv_two * gain_two_f).astype(bf16)

    (far,), (middle, inv_two, normed_two) = both_rounds(
        [gu_ring], [far_send()], mid, (tokens_f, gated, out_full)
    )
    far_take(far)

    def feed(normed, weight):
        pre = plain_dot(normed, weight)
        gate_pre, up_proj = pre[:, :fq], pre[:, fq:]
        return gate_pre, up_proj, (jax.nn.silu(gate_pre) * up_proj).astype(bf16)

    gu_q = [None] * 4
    fed = [None] * 4
    finish(gu_ring)
    gu_q[0] = gu_ring.rows()
    (far, gu_q[2]), fed[0] = both_rounds(
        [down_ring], [far_send(), (gu_q[0], to_core)], feed, (normed_two, gu_q[0])
    )
    far_take(far)
    (far,), fed[2] = both_rounds([down_ring], [far_send()], feed, (normed_two, gu_q[2]))
    far_take(far)

    def down_parts(cot, *hidden):
        return [cols_dot(h, cot) for h in hidden]

    (far,), (down_00, down_10) = both_rounds(
        [down_ring], [far_send()], down_parts, (cot, fed[0][2], fed[2][2])
    )
    far_take(far)
    (far, down_far), _ = both_rounds([down_ring], [far_send(), (down_10, to_core)])
    far_take(far)

    def column(value, b):
        n = order.index(b)
        return value[:, n * block : (n + 1) * block]

    def row(value, b):
        n = order.index(b)
        return value[n * block : (n + 1) * block]

    def col_scatter(mine, other, flip):
        return Scatter(lambda b: (column(mine, b), column(other, b)), flip)

    finish(down_ring)
    while len(far_pieces) < size:
        (far,), _ = ordered_round([far_send()])
        far_take(far)
    down_half = down_ring.cols()
    gu_q[1] = jnp.concatenate([far_pieces[b] for b in order], 0)
    down_s0 = col_scatter(down_00, down_far, True)
    (down_other, gu_q[3]), grad_h0 = both_rounds(
        [down_s0], [(down_half, to_core), (gu_q[1], to_core)], rows_dot, (cot, down_half)
    )
    down_h = (down_half, down_other)
    _, fed[1] = both_rounds([down_s0], (), feed, (normed_two, gu_q[1]))
    _, fed[3] = both_rounds([down_s0], (), feed, (normed_two, gu_q[3]))
    _, grad_h1 = both_rounds([down_s0], (), rows_dot, (cot, down_other))
    hidden_grad = [h[:, j * fq : (j + 1) * fq] for h in (grad_h0, grad_h1) for j in range(2)]

    def feed_back(grad, gate_pre, up_proj, normed):
        s = jax.nn.sigmoid(gate_pre)
        back = jnp.concatenate(
            [
                (grad * up_proj * s * (1.0 + gate_pre * (1.0 - s))).astype(bf16),
                (grad * gate_pre * s).astype(bf16),
            ],
            1,
        )
        return back, cols_dot(normed, back)

    def back_args(n):
        return (hidden_grad[n], fed[n][0], fed[n][1], normed_two)

    _, (back_3, local_3) = ordered_round([], feed_back, back_args(3))
    (gu_far_1,), (back_1, local_1) = ordered_round([(local_3, to_core)], feed_back, back_args(1))
    y_order = [size // 2]
    for step in range(size // 2 - 1, 0, -1):
        y_order += [size - step, step]
    y_order += [0]
    y_got = {}

    def y_send():
        b = y_order[len(y_got)]
        return (total(row(local_1, b), row(gu_far_1, b)), to_y)

    def y_take(value):
        y_got[y_order[len(y_got)]] = value

    (away,), (down_01, down_11) = ordered_round(
        [y_send()], down_parts, (cot, fed[1][2], fed[3][2])
    )
    y_take(away)
    (away, down_far_1), (back_2, local_2) = ordered_round(
        [y_send(), (down_11, to_core)], feed_back, back_args(2)
    )
    y_take(away)
    down_s1 = col_scatter(down_01, down_far_1, False)
    (away, gu_far_0), (back_0, local_0) = both_rounds(
        [down_s1], [y_send(), (local_2, to_core)], feed_back, back_args(0)
    )
    y_take(away)
    gu_s = Scatter(lambda b: (row(local_0, b), row(gu_far_0, b), y_got[b]), False)

    def through(b0, w0, b1, w1):
        return rows_dot(b0, w0) + rows_dot(b1, w1)

    (away,), grad_a = both_rounds(
        [down_s1, gu_s], [y_send()], through, (back_1, gu_q[1], back_3, gu_q[3])
    )
    y_take(away)

    def mid_back(grad_a, b0, w0, b1, w1, middle, inv_two, cot):
        grad = grad_a + rows_dot(b0, w0) + rows_dot(b1, w1)
        values, gain = norm_back(grad, middle, inv_two, gain_two_f)
        middle_grad = cot.astype(f32) + values
        return middle_grad, middle_grad.astype(bf16), gain

    (away,), (middle_grad, branch_back, gain_two_local) = both_rounds(
        [down_s1],
        [y_send()],
        mid_back,
        (grad_a, back_0, gu_q[0], back_2, gu_q[2], middle, inv_two, cot),
    )
    y_take(away)

    def gate_conv(branch_back, weight, gated):
        return cols_dot(gated, branch_back), rows_dot(branch_back, weight)

    (away,), (out_local, gated_grad) = both_rounds(
        [down_s1, gu_s], [y_send()], gate_conv, (branch_back, out_full, gated)
    )
    y_take(away)

    def conv_back(gated_grad, conv_out, c_part, b_part, x_part, mixed_in):
        c_grad = gated_grad * conv_out
        conv_grad_in = (gated_grad * c_part).reshape(-1, SEQ, width)
        conv_local = jnp.stack(
            [
                jnp.sum(conv_grad_in * shift_back(mixed_in, 2), (0, 1)),
                jnp.sum(conv_grad_in * shift_back(mixed_in, 1), (0, 1)),
                jnp.sum(conv_grad_in * mixed_in, (0, 1)),
            ],
            0,
        )
        mixed_grad = (
            taps[2] * conv_grad_in
            + taps[1] * shift_ahead(conv_grad_in, 1)
            + taps[0] * shift_ahead(conv_grad_in, 2)
        ).reshape(-1, width)
        b_back = (mixed_grad * x_part).astype(bf16)
        c_back = c_grad.astype(bf16)
        x_back = (mixed_grad * b_part).astype(bf16)

        def of_half(i):
            return jnp.concatenate(
                [
                    v[:, n * dq : (n + 1) * dq]
                    for n in (2 * i, 2 * i + 1)
                    for v in (b_back, c_back, x_back)
                ],
                1,
            )

        return conv_local, of_half(0), of_half(1)

    half = out_local.shape[0] // 2
    (away, out_got), (conv_local, in_back_0, in_back_1) = ordered_round(
        [y_send(), (out_local[half:], to_core)],
        conv_back,
        (gated_grad, conv_out, c_part, b_part, x_part, mixed_in),
    )
    y_take(away)
    out_s = col_scatter(out_local[:half], out_got, True)

    def in_parts(normed_one, back_0, back_1):
        return cols_dot(normed_one, back_0), cols_dot(normed_one, back_1)

    (away,), (in_local_0, in_local_1) = both_rounds(
        [gu_s, out_s], [y_send()], in_parts, (normed_one, in_back_0, in_back_1)
    )
    y_take(away)

    def first_back(b0, w0, b1, w1, tokens_f, inv_one, middle_grad):
        grad = through(b0, w0, b1, w1)
        values, gain = norm_back(grad, tokens_f, inv_one, gain_one_f)
        return (middle_grad + values).astype(bf16), gain

    (in_far_0,), (tokens_grad, gain_one_local) = both_rounds(
        [gu_s, out_s],
        [(in_local_1, to_core)],
        first_back,
        (in_back_0, in_h[0], in_back_1, in_h[1], tokens_f, inv_one, middle_grad),
    )

    conv_rel = lax.dot_general(
        conv_local.astype(bf16), to_feature, (((1,), (1,)), ((), ())), preferred_element_type=f32
    ).astype(bf16)
    small_grad = jnp.concatenate(
        [gain_one_local.astype(bf16)[None], gain_two_local.astype(bf16)[None], conv_rel], 0
    )
    small_rows = small_grad.reshape(5, size, block).transpose(1, 0, 2).reshape(size, 5 * block)
    small_rows = jnp.pad(small_rows, ((0, PACK - size), (0, 6 * dq - 5 * block)))

    def in_block(b):
        n = order.index(b)
        small = jnp.pad(small_rows[n : n + 1], ((0, PACK - 1), (0, 0)))
        far = jnp.pad(small_far[n : n + 1], ((0, PACK - 1), (0, 0)))
        return (
            jnp.concatenate([row(in_local_0, b), small], 0),
            jnp.concatenate([row(in_far_0, b), far], 0),
        )

    small_far = send(small_rows, to_core)
    in_s = Scatter(in_block, False)
    while len(y_got) < size:
        (away,), _ = ordered_round([y_send()])
        y_take(away)
    finish(gu_s)
    gu_slice = gu_s.result()

    def block_sum(middle, h0, h1, h2, h3, w0, w1):
        return (
            middle
            + plain_dot(jnp.concatenate([h0, h1], 1), w0)
            + plain_dot(jnp.concatenate([h2, h3], 1), w1)
        ).astype(bf16)

    (gu_other,), block_out = both_rounds(
        [in_s, out_s],
        [(gu_slice, to_y)],
        block_sum,
        (middle, *[f[2] for f in fed], *down_h),
    )
    both_rounds([in_s, out_s])
    both_rounds([in_s])
    both_rounds([in_s])
    finish(in_s, out_s, down_s0, down_s1)
    down_slice = jnp.concatenate([down_s0.result(), down_s1.result()], 0)
    out_slice = out_s.result()
    in_slice = in_s.result()

    def over_y(value):
        return high_reps(add(value, send(value, to_y)))

    def swap(flag, first, second, axis):
        return jnp.where(
            flag == 0,
            jnp.concatenate([first, second], axis),
            jnp.concatenate([second, first], axis),
        )

    def y_ordered(value, axis):
        n = value.shape[axis] // 2
        return swap(
            ybit,
            lax.slice_in_dim(value, 0, n, axis=axis),
            lax.slice_in_dim(value, n, 2 * n, axis=axis),
            axis,
        )

    def whole(value):
        total = over_y(y_ordered(value, 0))
        return swap(core, total, send(total, to_core), 0).astype(f32)

    down_grad = whole(down_slice)
    out_grad = whole(out_slice)
    in_total = over_y(
        jnp.concatenate([y_ordered(in_slice[:block], 1), in_slice[block:]], 0)
    )
    in_mine_total = in_total[:block].reshape(block, 2, 3, dq)
    in_other_total = send(in_total[:block], to_core).reshape(block, 2, 3, dq)
    in_grad = (
        swap(core, in_mine_total, in_other_total, 1)
        .transpose(0, 2, 1, 3)
        .reshape(block, 3 * width)
        .astype(f32)
    )
    small_total = in_total[block, : 5 * block].astype(f32).reshape(5, block)
    gu_total = high_reps(gu_slice)
    gu_other = high_reps(gu_other)
    gu_both = jnp.stack([gu_total, gu_other], 0)
    gu_far = send(gu_both, to_core)

    def gu_out(start):
        own = swap(ybit, gu_both[0][:, start : start + fq], gu_both[1][:, start : start + fq], 1)
        far = swap(ybit, gu_far[0][:, start : start + fq], gu_far[1][:, start : start + fq], 1)
        return swap(core, own, far, 1).astype(f32)

    gate_grad, up_grad = gu_out(0), gu_out(fq)

    def to_natural(value):
        return rows_dot(value, to_rel).astype(bf16)

    return (
        to_natural(block_out),
        to_natural(tokens_grad),
        small_total[0],
        in_grad,
        small_total[2:],
        out_grad,
        small_total[1],
        gate_grad,
        up_grad,
        down_grad,
    )


def solution(mesh):
    in_specs = (
        P(("rep", "shard"), None),
        P("shard"),
        P("shard", None),
        P(None, "shard"),
        P(None, "shard"),
        P("shard"),
        P("shard", None),
        P("shard", None),
        P(None, "shard"),
        P(("rep", "shard"), None),
    )
    out_specs = (
        P(("rep", "shard"), None),
        P(("rep", "shard"), None),
        P("shard"),
        P("shard", None),
        P(None, "shard"),
        P(None, "shard"),
        P("shard"),
        P("shard", None),
        P("shard", None),
        P(None, "shard"),
    )
    body = functools.partial(shards, mesh.shape["rep"], mesh.shape["shard"])
    return jax.shard_map(body, mesh=mesh, in_specs=in_specs, out_specs=out_specs, check_vma=False)
```

```python
import functools

import jax
import jax.numpy as jnp
from jax import lax
from jax.experimental import pallas as pl
from jax.experimental.pallas import tpu as pltpu
from jax.sharding import PartitionSpec as P

SEQ = 512


EPSILON = 1e-05

AXES = ("rep", "shard")
PACK = 16


def plain_dot(left, right, kind=jnp.float32):
    return jnp.dot(left, right, preferred_element_type=jnp.float32).astype(kind)


def rows_dot(left, right):
    return lax.dot_general(
        left, right, (((1,), (1,)), ((), ())), preferred_element_type=jnp.float32
    )


def cols_dot(left, right):
    return lax.dot_general(
        left, right, (((0,), (0,)), ((), ())), preferred_element_type=jnp.float32
    ).astype(jnp.bfloat16)


def kernel_call(body, steps, ins, outs):
    return pl.pallas_call(
        body,
        grid=(steps,),
        in_specs=[pl.BlockSpec(block, where) for _, block, where in ins],
        out_specs=[pl.BlockSpec(block, where) for _, _, block, where in outs],
        out_shape=[jax.ShapeDtypeStruct(shape, kind) for shape, kind, _, _ in outs],
        compiler_params=pltpu.CompilerParams(vmem_limit_bytes=56 * 2**20),
    )(*[v for v, _, _ in ins])


def same(n):
    return (0, 0)


def columns(n):
    return (0, n)


def rows(n):
    return (n, 0)


def gathered(piece_refs, weight_ref):
    extent = piece_refs[0].shape[0]
    for n, piece_ref in enumerate(piece_refs):
        weight_ref[n * extent : (n + 1) * extent, :] = piece_ref[...]


def feed(normed, pieces, tiles):
    count, depth = normed.shape
    extent = depth // len(pieces)
    pair = pieces[0].shape[1] // tiles
    tile = pair // 2

    def body(normed_ref, *refs):
        *piece_refs, pre_ref, hidden_ref, weight_ref = refs
        gathered(piece_refs, weight_ref)
        pre = jnp.dot(normed_ref[...], weight_ref[...], preferred_element_type=jnp.float32)
        pre_ref[...] = pre.astype(jnp.bfloat16)
        gate = pre[:, :tile]
        hidden_ref[...] = (gate * jax.nn.sigmoid(gate) * pre[:, tile:]).astype(jnp.bfloat16)

    return kernel_call(
        body,
        tiles,
        [(normed, (count, depth), same)] + [(v, (extent, pair), columns) for v in pieces],
        [
            ((count, tiles * pair), jnp.bfloat16, (count, pair), columns),
            ((count, tiles * tile), jnp.bfloat16, (count, tile), columns),
            ((depth, tiles * pair), jnp.bfloat16, (depth, pair), columns),
        ],
    )


def feed_back(cot, down_rows, pre, normed, tiles, first):
    count, depth = cot.shape
    pair = pre.shape[1] // tiles
    tile = pair // 2

    def body(cot_ref, down_ref, pre_ref, normed_ref, back_ref, local_ref):
        grad = rows_dot(cot_ref[...], down_ref[...])
        gate = pre_ref[:, :tile].astype(jnp.float32)
        up = pre_ref[:, tile:].astype(jnp.float32)
        sigma = jax.nn.sigmoid(gate)
        back_ref[:, :tile] = (grad * up * sigma * (1.0 + gate * (1.0 - sigma))).astype(jnp.bfloat16)
        back_ref[:, tile:] = (grad * gate * sigma).astype(jnp.bfloat16)
        local_ref[...] = cols_dot(normed_ref[...], back_ref[...])

    return kernel_call(
        body,
        tiles,
        [
            (cot, (count, depth), same),
            (down_rows, (tile, depth), lambda n: (n + first, 0)),
            (pre, (count, pair), columns),
            (normed, (count, depth), same),
        ],
        [
            ((count, tiles * pair), jnp.bfloat16, (count, pair), columns),
            ((depth, tiles * pair), jnp.bfloat16, (depth, pair), columns),
        ],
    )


def shifted(values, steps):
    count = values.shape[0]
    at = lax.broadcasted_iota(jnp.int32, values.shape, 0) % SEQ
    inside = (at >= steps) & (at < SEQ + steps)
    return jnp.where(inside, pltpu.roll(values, steps % count, 0), 0.0)


def convolve(normed, pieces, taps, tiles):
    count, depth = normed.shape
    extent = depth // len(pieces)
    triple = pieces[0].shape[1] // tiles
    tile = triple // 3

    def body(normed_ref, taps_ref, *refs):
        *piece_refs, parts_ref, gated_ref, weight_ref = refs
        gathered(piece_refs, weight_ref)
        parts = jnp.dot(normed_ref[...], weight_ref[...], preferred_element_type=jnp.float32)
        parts_ref[...] = parts.astype(jnp.bfloat16)
        mixed = parts[:, :tile] * parts[:, 2 * tile :]
        conv = (
            taps_ref[0:1, :] * shifted(mixed, 2)
            + taps_ref[1:2, :] * shifted(mixed, 1)
            + taps_ref[2:3, :] * mixed
        )
        gated_ref[...] = (parts[:, tile : 2 * tile] * conv).astype(jnp.bfloat16)

    return kernel_call(
        body,
        tiles,
        [(normed, (count, depth), same), (taps, (3, tile), columns)]
        + [(v, (extent, triple), columns) for v in pieces],
        [
            ((count, tiles * triple), jnp.bfloat16, (count, triple), columns),
            ((count, tiles * tile), jnp.bfloat16, (count, tile), columns),
            ((depth, tiles * triple), jnp.bfloat16, (depth, triple), columns),
        ],
    )


def convolve_back(branch_back, out_rows, parts, gated, taps, normed, tiles):
    count, depth = branch_back.shape
    triple = parts.shape[1] // tiles
    tile = triple // 3

    def body(
        branch_ref, out_ref, parts_ref, gated_ref, taps_ref, normed_ref,
        back_ref, local_ref, taps_local_ref,
    ):
        gated_grad = rows_dot(branch_ref[...], out_ref[...])
        b_part = parts_ref[:, :tile].astype(jnp.float32)
        c_part = parts_ref[:, tile : 2 * tile].astype(jnp.float32)
        x_part = parts_ref[:, 2 * tile :].astype(jnp.float32)
        mixed = b_part * x_part
        before_1, before_2 = shifted(mixed, 1), shifted(mixed, 2)
        conv = (
            taps_ref[0:1, :] * before_2 + taps_ref[1:2, :] * before_1 + taps_ref[2:3, :] * mixed
        )
        conv_grad = gated_grad * c_part
        taps_local_ref[...] = jnp.concatenate(
            [
                jnp.sum(conv_grad * before_2, 0, keepdims=True),
                jnp.sum(conv_grad * before_1, 0, keepdims=True),
                jnp.sum(conv_grad * mixed, 0, keepdims=True),
            ],
            0,
        )
        mixed_grad = (
            taps_ref[2:3, :] * conv_grad
            + taps_ref[1:2, :] * shifted(conv_grad, -1)
            + taps_ref[0:1, :] * shifted(conv_grad, -2)
        )
        back_ref[:, :tile] = (mixed_grad * x_part).astype(jnp.bfloat16)
        back_ref[:, tile : 2 * tile] = (gated_grad * conv).astype(jnp.bfloat16)
        back_ref[:, 2 * tile :] = (mixed_grad * b_part).astype(jnp.bfloat16)
        local_ref[:, :triple] = cols_dot(normed_ref[...], back_ref[...])
        local_ref[:, triple:] = cols_dot(branch_ref[...], gated_ref[...])

    return kernel_call(
        body,
        tiles,
        [
            (branch_back, (count, depth), same),
            (out_rows, (tile, depth), rows),
            (parts, (count, triple), columns),
            (gated, (count, tile), columns),
            (taps, (3, tile), columns),
            (normed, (count, depth), same),
        ],
        [
            ((count, tiles * triple), jnp.bfloat16, (count, triple), columns),
            ((depth, tiles * 4 * tile), jnp.bfloat16, (depth, 4 * tile), columns),
            ((3, tiles * tile), jnp.float32, (3, tile), columns),
        ],
    )


def norm_back(extra, backs, weights, values, inv_rms, gain, base, width):
    count, depth = values.shape
    total = len(backs)
    per = backs[0].shape[1] // width
    rows_at_once = min(128, count)
    operands = [] if extra is None else [extra]

    def at(q):
        return lambda n: (0, jnp.clip(n - q * per, 0, per - 1))

    def body(*refs):
        back_refs, weight_refs = refs[:total], refs[total : 2 * total]
        values_ref, inv_ref, gain_ref, base_ref = refs[2 * total : 2 * total + 4]
        extra_refs = refs[2 * total + 4 : -3]
        out_ref, gain_grad_ref, sum_ref = refs[-3:]
        n = pl.program_id(0)

        @pl.when(n == 0)
        def _():
            first = rows_dot(back_refs[0][...], weight_refs[0][...])
            sum_ref[...] = first + extra_refs[0][...] if extra_refs else first

        for q in range(total):

            @pl.when((n // per == q) & (n != 0))
            def _(q=q):
                sum_ref[...] += rows_dot(back_refs[q][...], weight_refs[q][...])

        @pl.when(n == total * per - 1)
        def _():
            def some_rows(at_chunk, gain_grad):
                here = pl.ds(pl.multiple_of(at_chunk * rows_at_once, rows_at_once), rows_at_once)
                grad = sum_ref[here, :]
                scaled = grad * gain_ref[...]
                held = values_ref[here, :].astype(jnp.float32)
                inv = inv_ref[here, :]
                mean = jnp.mean(scaled * held, -1, keepdims=True)
                made = inv * (scaled - held * (inv * inv * mean))
                out_ref[here, :] = (base_ref[here, :].astype(jnp.float32) + made).astype(
                    jnp.bfloat16
                )
                return gain_grad + jnp.sum(grad * held * inv, 0, keepdims=True)

            gain_grad_ref[...] = lax.fori_loop(
                0, count // rows_at_once, some_rows, jnp.zeros((1, depth), jnp.float32)
            )

    return pl.pallas_call(
        body,
        grid=(total * per,),
        in_specs=[pl.BlockSpec((count, width), at(q)) for q in range(total)]
        + [pl.BlockSpec((depth, width), at(q)) for q in range(total)]
        + [
            pl.BlockSpec((count, depth), same),
            pl.BlockSpec((count, 1), same),
            pl.BlockSpec((1, depth), same),
            pl.BlockSpec((count, depth), same),
        ]
        + [pl.BlockSpec((count, depth), same) for _ in operands],
        out_specs=[pl.BlockSpec((count, depth), same), pl.BlockSpec((1, depth), same)],
        out_shape=[
            jax.ShapeDtypeStruct((count, depth), jnp.bfloat16),
            jax.ShapeDtypeStruct((1, depth), jnp.float32),
        ],
        scratch_shapes=[pltpu.VMEM((count, depth), jnp.float32)],
        compiler_params=pltpu.CompilerParams(vmem_limit_bytes=56 * 2**20),
    )(*backs, *weights, values, inv_rms, gain[None, :], base, *operands)


def in_order(core, mine, other, quarter):
    block = mine.shape[0]

    def body(core_ref, mine_ref, other_ref, in_ref, out_ref):
        first = core_ref[0, 0] == 0
        halves = [
            jnp.where(first, mine_ref[...], other_ref[...]).astype(jnp.float32),
            jnp.where(first, other_ref[...], mine_ref[...]).astype(jnp.float32),
        ]
        for at in range(4):
            start = (at % 2) * 4 * quarter
            parts = halves[at // 2][:, start : start + 4 * quarter]
            for n in range(3):
                to = (4 * n + at) * quarter
                in_ref[:, to : to + quarter] = parts[:, n * quarter : (n + 1) * quarter]
            out_ref[at * quarter : (at + 1) * quarter, :] = parts[:, 3 * quarter :].T

    return pl.pallas_call(
        body,
        in_specs=[
            pl.BlockSpec(memory_space=pltpu.SMEM),
            pl.BlockSpec(memory_space=pltpu.VMEM),
            pl.BlockSpec(memory_space=pltpu.VMEM),
        ],
        out_specs=[pl.BlockSpec(memory_space=pltpu.VMEM)] * 2,
        out_shape=[
            jax.ShapeDtypeStruct((block, 12 * quarter), jnp.float32),
            jax.ShapeDtypeStruct((4 * quarter, block), jnp.float32),
        ],
        compiler_params=pltpu.CompilerParams(vmem_limit_bytes=56 * 2**20),
    )(core.astype(jnp.int32).reshape(1, 1), mine, other)


def cycle_of(size):
    wide = size // 4
    walk = [(0, 0)]
    for row in range(4):
        cols = range(1, wide)
        walk += [(row, col) for col in (cols if row % 2 == 0 else reversed(cols))]
    walk += [(row, 0) for row in (3, 2, 1)]
    return [row * wide + col for row, col in walk]


def shards(
    reps,
    size,
    tokens,
    norm_gain_one,
    in_weight,
    conv_weight,
    out_weight,
    norm_gain_two,
    gate_weight,
    up_weight,
    down_weight,
    cotangent,
):
    bf16, f32 = jnp.bfloat16, jnp.float32
    width = tokens.shape[1]
    hidden_width = gate_weight.shape[1]
    block = width // size
    fq, dq = hidden_width // 4, width // 4
    tiles = 3 if fq % 384 == 0 else 1
    tile = fq // tiles
    ring = cycle_of(size)
    place = [ring.index(s) for s in range(size)]

    def pairs(move):
        return [
            (r * size + s, move(r, s)[0] * size + move(r, s)[1])
            for r in range(reps)
            for s in range(size)
        ]

    cw = pairs(lambda r, s: (r, ring[(place[s] + 1) % size]))
    ccw = pairs(lambda r, s: (r, ring[(place[s] - 1) % size]))
    to_core = pairs(lambda r, s: (r ^ 1, s))
    to_y = pairs(lambda r, s: (r ^ 2, s))

    def send(value, perm):
        return lax.ppermute(value, AXES, perm)

    rep = lax.axis_index("rep")
    core, ybit = rep % 2, (rep // 2) % 2
    at = jnp.asarray(place)[lax.axis_index("shard")]

    order = [0]
    for step in range(1, size // 2):
        order += [step, size - step]
    order += [size // 2]
    natural_block = jnp.asarray(ring)[(at - jnp.asarray(order)) % size]
    natural = (natural_block[:, None] * block + jnp.arange(block)[None, :]).reshape(-1)
    to_rel = (jnp.arange(width)[:, None] == natural[None, :]).astype(bf16)

    def quarter(i, j):
        return (core ^ i) * 2 + (ybit ^ j)

    quarters = ((0, 0), (0, 1), (1, 0), (1, 1))
    natural_feature = (
        jnp.stack([quarter(i, j) for i, j in quarters])[:, None] * dq + jnp.arange(dq)[None, :]
    ).reshape(-1)

    last = []

    def ordered_round(sends, work=None, args=()):
        leaves, tree = jax.tree.flatten(([v for v, _ in sends], tuple(args)))
        held = lax.optimization_barrier(tuple(leaves) + tuple(last))
        values, args = jax.tree.unflatten(tree, held[: len(leaves)])
        got = [send(v, perm) for v, (_, perm) in zip(values, sends)]
        made = work(*args) if work is not None else None
        last[:] = got + jax.tree.leaves(made)
        return got, made

    class Gather:
        def __init__(self, piece, flip):
            self.got = {0: piece}
            self.n_cw = size // 2 - (1 if flip else 0)
            self.n_ccw = size - 1 - self.n_cw
            self.step = 0

        def sends(self):
            self.step += 1
            self.to = []
            out = []
            if self.step <= self.n_cw:
                out.append((self.got[self.step - 1], cw))
                self.to.append(self.step)
            if self.step <= self.n_ccw:
                out.append((self.got[(size - self.step + 1) % size], ccw))
                self.to.append(size - self.step)
            return out

        def take(self, got):
            for b in self.to:
                self.got[b] = got.pop(0)

        def done(self):
            return self.step == size // 2

        def rows(self):
            return jnp.concatenate([self.got[b] for b in order], 0)

        def cols(self):
            return jnp.concatenate([self.got[b] for b in order], 1)

    class Scatter:
        def __init__(self, own, flip):
            self.own = own
            self.n_cw = size // 2 - (1 if flip else 0)
            self.n_ccw = size - 1 - self.n_cw
            self.step = size // 2 + 1
            self.up = self.down = None

        def sends(self):
            self.step -= 1
            out = []
            if self.step <= self.n_cw:
                out.append((total(*self.own(size - self.step), self.up), cw))
            if self.step <= self.n_ccw:
                out.append((total(*self.own(self.step), self.down), ccw))
            return out

        def take(self, got):
            if self.step <= self.n_cw:
                self.up = got.pop(0)
            if self.step <= self.n_ccw:
                self.down = got.pop(0)

        def done(self):
            return self.step == 1

        def result(self):
            return total(*self.own(0), self.up, self.down)

    def total(*values):
        values = [v for v in values if v is not None]
        if len(values) == 1:
            return values[0]
        return sum(v.astype(f32) for v in values).astype(bf16)

    def add(left, right):
        return total(left, right)

    def both_rounds(rings, others=(), work=None, args=()):
        sends = []
        counts = []
        for r in rings:
            mine = r.sends()
            counts.append(len(mine))
            sends += mine
        got, made = ordered_round(sends + list(others), work, args)
        for r, n in zip(rings, counts):
            r.take(got[:n])
            got = got[n:]
        return got, made

    def finish(*rings):
        while rings := [r for r in rings if not r.done()]:
            both_rounds(rings)

    def high_reps(value):
        step = 4
        while step < reps:
            other = send(value, pairs(lambda r, s: (r ^ step, s)))
            value = (value.astype(f32) + other.astype(f32)).astype(value.dtype)
            step *= 2
        return value

    def part(value, axis, i, j, extent):
        return lax.dynamic_slice_in_dim(value, quarter(i, j) * extent, extent, axis)

    def in_part(i, j):
        return part(in_weight.reshape(block, 3, width), 2, i, j, dq).reshape(block, 3 * dq)

    def gu_part(gate_weight, up_weight, i, j):
        both = [part(gate_weight, 1, i, j, fq), part(up_weight, 1, i, j, fq)]
        return jnp.concatenate(
            [w[:, t * tile : (t + 1) * tile] for t in range(tiles) for w in both], 1
        )

    def half_part(value):
        extent = value.shape[0] // 4
        return jnp.concatenate([part(value, 0, 0, j, extent) for j in range(2)], 0)

    small = jnp.concatenate([norm_gain_one, norm_gain_two, conv_weight.reshape(-1)])
    pack = jnp.pad(small[None, :], ((0, PACK - 1), (0, 6 * dq - small.shape[0])))
    in_ring = Gather(
        jnp.concatenate([jnp.concatenate([in_part(0, 0), in_part(0, 1)], 1), pack], 0), False
    )
    far_order = [b for b in order if b != 0]

    def far_send():
        b = far_order[len(far_pieces) - 1]
        return (gu_ring.got[b], to_y)

    def far_take(value):
        far_pieces[far_order[len(far_pieces) - 1]] = value

    def prepare(tokens, gate_weight, up_weight):
        tokens_rel = plain_dot(tokens, to_rel, bf16)
        values = tokens_rel.astype(f32)
        inv_one = lax.rsqrt(jnp.mean(values * values, -1, keepdims=True) + EPSILON)
        return tokens_rel, inv_one

    _, out_own = both_rounds([in_ring], (), half_part, (out_weight,))
    out_ring = Gather(out_own, True)
    _, (tokens_rel, inv_one) = both_rounds(
        [in_ring, out_ring], (), prepare, (tokens, gate_weight, up_weight)
    )
    _, gu_own = both_rounds(
        [in_ring, out_ring], (), lambda g, u: gu_part(g, u, 0, 0), (gate_weight, up_weight)
    )
    gu_ring = Gather(gu_own, True)
    _, far_own = both_rounds(
        [in_ring, out_ring], (), lambda g, u: gu_part(g, u, 0, 1), (gate_weight, up_weight)
    )
    far_pieces = {0: far_own}
    finish(in_ring)
    in_pieces = [in_ring.got[b] for b in order]
    packs = jnp.stack([v[block, : 5 * block] for v in in_pieces], 0).reshape(size, 5, block)
    gain_one_f = packs[:, 0].reshape(-1).astype(f32)
    gain_two_f = packs[:, 1].reshape(-1).astype(f32)
    to_feature = (natural[:, None] == natural_feature[None, :]).astype(bf16)
    taps = plain_dot(packs[:, 2:].transpose(1, 0, 2).reshape(3, width), to_feature)
    taps_h = (taps[:, : 2 * dq], taps[:, 2 * dq :])

    def project_first(tokens_rel, inv_one, gain, taps, *pieces):
        normed_one = (tokens_rel.astype(f32) * inv_one * gain).astype(bf16)
        return normed_one, convolve(normed_one, pieces, taps, 2)

    _, (normed_one, (parts_0, gated_0, in_half)) = both_rounds(
        [gu_ring, out_ring],
        (),
        project_first,
        (tokens_rel, inv_one, gain_one_f, taps_h[0], *in_pieces),
    )

    def prepare_more(cotangent, down_weight):
        return plain_dot(cotangent, to_rel, bf16), half_part(down_weight)

    finish(out_ring)
    out_half = out_ring.cols()
    (far, in_far, out_far), (cot, down_own) = both_rounds(
        [gu_ring],
        [far_send(), (in_half, to_core), (out_half, to_core)],
        prepare_more,
        (cotangent, down_weight),
    )
    far_take(far)
    down_ring = Gather(down_own, False)
    in_h = (in_half, in_far)

    def project_second(normed_one, weight, taps):
        return convolve(normed_one, [weight], taps, 2)[:2]

    (far,), (parts_1, gated_1) = both_rounds(
        [gu_ring], [far_send()], project_second, (normed_one, in_far, taps_h[1])
    )
    far_take(far)
    parts_h, gated_h = (parts_0, parts_1), (gated_0, gated_1)

    def mid(tokens_rel, g0, w0, g1, w1):
        middle = tokens_rel.astype(f32) + plain_dot(g0, w0) + plain_dot(g1, w1)
        inv_two = lax.rsqrt(jnp.mean(middle * middle, -1, keepdims=True) + EPSILON)
        return middle, inv_two, (middle * inv_two * gain_two_f).astype(bf16)

    gu_q = [None] * 4
    fed = [None] * 4

    def feed_tiles(normed, *pieces):
        return feed(normed, pieces, tiles)

    out_h = (out_half, out_far)
    (far,), (middle, inv_two, normed_two) = both_rounds(
        [gu_ring], [far_send()], mid, (tokens_rel, gated_0, out_half, gated_1, out_far)
    )
    far_take(far)
    finish(gu_ring)
    (far,), fed[0] = both_rounds(
        [down_ring], [far_send()], feed_tiles, (normed_two, *[gu_ring.got[b] for b in order])
    )
    far_take(far)
    gu_q[0] = fed[0][2]

    def down_parts(cot, *hidden):
        return [cols_dot(h, cot) for h in hidden]

    (far, gu_q[2]), (down_00,) = both_rounds(
        [down_ring], [far_send(), (gu_q[0], to_core)], down_parts, (cot, fed[0][1])
    )
    far_take(far)
    (far,), fed[2] = both_rounds([down_ring], [far_send()], feed_tiles, (normed_two, gu_q[2]))
    far_take(far)
    (far,), (down_10,) = both_rounds(
        [down_ring], [far_send()], down_parts, (cot, fed[2][1])
    )
    far_take(far)

    def column(value, b):
        n = order.index(b)
        return value[:, n * block : (n + 1) * block]

    def row(value, b):
        n = order.index(b)
        return value[n * block : (n + 1) * block]

    def col_scatter(mine, other, flip):
        return Scatter(lambda b: (column(mine, b), column(other, b)), flip)

    finish(down_ring)
    while len(far_pieces) < size:
        (far,), _ = ordered_round([far_send()])
        far_take(far)
    down_half = down_ring.cols()
    (down_other, down_far), fed[1] = ordered_round(
        [(down_half, to_core), (down_10, to_core)],
        feed_tiles,
        (normed_two, *[far_pieces[b] for b in order]),
    )
    gu_q[1] = fed[1][2]
    down_s0 = col_scatter(down_00, down_far, True)
    down_h = (down_half, down_other)
    (gu_q[3],), (down_01,) = both_rounds(
        [down_s0], [(gu_q[1], to_core)], down_parts, (cot, fed[1][1])
    )
    _, fed[3] = both_rounds([down_s0], (), feed_tiles, (normed_two, gu_q[3]))

    def feed_back_first(cot, down_rows, pre, normed):
        return feed_back(cot, down_rows, pre, normed, tiles, 0)

    def feed_back_second(cot, down_rows, pre, normed):
        return feed_back(cot, down_rows, pre, normed, tiles, tiles)

    def back_args(n):
        return (cot, down_h[n // 2], fed[n][0], normed_two)

    _, (back_3, local_3) = both_rounds([down_s0], (), feed_back_second, back_args(3))
    (gu_far_1,), (back_1, local_1) = both_rounds(
        [down_s0], [(local_3, to_core)], feed_back_second, back_args(1)
    )
    y_order = [size // 2]
    for step in range(size // 2 - 1, 0, -1):
        y_order += [size - step, step]
    y_order += [0]
    y_got = {}

    def y_send():
        b = y_order[len(y_got)]
        return (total(row(local_1, b), row(gu_far_1, b)), to_y)

    def y_take(value):
        y_got[y_order[len(y_got)]] = value


    def down_part_and_sum(cot, h3, middle, h0, h1, weight):
        half = middle + plain_dot(jnp.concatenate([h0, h1], 1), weight)
        return cols_dot(h3, cot), half

    (away,), (down_11, half_out) = ordered_round(
        [y_send()], down_part_and_sum, (cot, fed[3][1], middle, fed[0][1], fed[1][1], down_half)
    )
    y_take(away)
    (away, down_far_1), (back_2, local_2) = ordered_round(
        [y_send(), (down_11, to_core)], feed_back_first, back_args(2)
    )
    y_take(away)
    down_s1 = col_scatter(down_01, down_far_1, False)
    (away, gu_far_0), (back_0, local_0) = both_rounds(
        [down_s1], [y_send(), (local_2, to_core)], feed_back_first, back_args(0)
    )
    y_take(away)
    gu_s = Scatter(lambda b: (row(local_0, b), row(gu_far_0, b), y_got[b]), False)

    def through(b0, w0, b1, w1):
        return rows_dot(b0, w0) + rows_dot(b1, w1)

    (away,), grad_a = both_rounds(
        [down_s1, gu_s], [y_send()], through, (back_1, gu_q[1], back_3, gu_q[3])
    )
    y_take(away)

    def mid_back(grad_a, b0, w0, b1, w1, middle, inv_two, gain, cot):
        return norm_back(grad_a, [b0, b1], [w0, w1], middle, inv_two, gain, cot, 2 * tile)

    (away,), (branch_back, gain_two_local) = both_rounds(
        [down_s1],
        [y_send()],
        mid_back,
        (grad_a, back_0, gu_q[0], back_2, gu_q[2], middle, inv_two, gain_two_f, cot),
    )
    y_take(away)

    def conv_back_half(branch_back, out_rows, parts, gated, taps, normed_one):
        return convolve_back(branch_back, out_rows, parts, gated, taps, normed_one, 2)

    def conv_args(i):
        return (branch_back, out_h[i], parts_h[i], gated_h[i], taps_h[i], normed_one)

    (away,), (in_back_1, in_local_1, taps_local_1) = both_rounds(
        [down_s1, gu_s], [y_send()], conv_back_half, conv_args(1)
    )
    y_take(away)
    (away, in_got), (in_back_0, in_local_0, taps_local_0) = both_rounds(
        [gu_s], [y_send(), (in_local_1, to_core)], conv_back_half, conv_args(0)
    )
    y_take(away)
    in_s = Scatter(lambda b: (row(in_local_0, b), row(in_got, b)), False)

    def swap(flag, first, second, axis):
        return jnp.where(
            flag == 0,
            jnp.concatenate([first, second], axis),
            jnp.concatenate([second, first], axis),
        )

    def y_ordered(value, axis):
        n = value.shape[axis] // 2
        return swap(
            ybit,
            lax.slice_in_dim(value, 0, n, axis=axis),
            lax.slice_in_dim(value, n, 2 * n, axis=axis),
            axis,
        )

    finish(down_s0, down_s1)
    down_slice = y_ordered(jnp.concatenate([down_s0.result(), down_s1.result()], 0), 0)

    def first_back(b0, w0, b1, w1, tokens_rel, inv_one, gain, branch_back):
        return norm_back(
            None, [b0, b1], [w0, w1], tokens_rel, inv_one, gain, branch_back, 3 * dq
        )

    (away, down_got), (tokens_grad, gain_one_local) = both_rounds(
        [gu_s, in_s],
        [y_send(), (down_slice, to_y)],
        first_back,
        (in_back_0, in_h[0], in_back_1, in_h[1], tokens_rel, inv_one, gain_one_f, branch_back),
    )
    y_take(away)

    def to_natural(value):
        return rows_dot(value.astype(bf16), to_rel)

    def small_start(gain_one_local, gain_two_local, taps_0, taps_1):
        conv_natural = rows_dot(
            jnp.concatenate([taps_0, taps_1], 1).astype(bf16),
            (jnp.arange(width)[:, None] == natural_feature[None, :]).astype(bf16),
        )
        gains = to_natural(jnp.concatenate([gain_one_local, gain_two_local], 0))
        return jnp.concatenate([gains, conv_natural], 0)

    small_moves = []
    step = 1
    while step < size:
        small_moves.append(pairs(lambda r, s, step=step: (r, s ^ step)))
        step *= 2

    def small_send():
        return (small_sum, small_moves.pop(0))

    while len(y_got) < size:
        (away,), _ = ordered_round([y_send()])
        y_take(away)
    finish(gu_s)
    gu_slice = gu_s.result()

    def block_sum(half_out, h2, h3, weight):
        return (half_out + plain_dot(jnp.concatenate([h2, h3], 1), weight)).astype(bf16)

    gu_slice = high_reps(gu_slice)
    down_total = high_reps(add(down_slice, down_got))
    def block_sum_and_small(half_out, h2, h3, weight, *small):
        return block_sum(half_out, h2, h3, weight), small_start(*small)

    (down_away, gu_other), (block_out, small_sum) = both_rounds(
        [in_s],
        [(down_total, to_core), (gu_slice, to_y)],
        block_sum_and_small,
        (
            half_out, fed[2][1], fed[3][1], down_other,
            gain_one_local, gain_two_local, taps_local_0, taps_local_1,
        ),
    )
    gu_both = jnp.stack([gu_slice, gu_other], 0)
    (small_got, gu_far), natural_outs = both_rounds(
        [in_s],
        [small_send(), (gu_both, to_core)],
        lambda *vs: [to_natural(v).astype(bf16) for v in vs],
        (block_out, tokens_grad),
    )
    small_sum = small_sum + small_got

    def core_whole(mine, other, axis):
        return swap(core, mine, other, axis).astype(f32)

    def gu_out(start):
        def of(value):
            return jnp.concatenate(
                [value[:, (2 * t + start) * tile : (2 * t + start + 1) * tile] for t in range(tiles)], 1
            )

        own = swap(ybit, of(gu_both[0]), of(gu_both[1]), 1)
        far = swap(ybit, of(gu_far[0]), of(gu_far[1]), 1)
        return core_whole(own, far, 1)

    def down_gate_up(down_total, down_away):
        return core_whole(down_total, down_away, 0), gu_out(0), gu_out(1)

    (small_got,), (down_grad, gate_grad, up_grad) = both_rounds(
        [in_s], [small_send()], down_gate_up, (down_total, down_away)
    )
    small_sum = small_sum + small_got
    finish(in_s)
    in_slice = y_ordered(in_s.result(), 1)
    (small_got, in_got), _ = ordered_round([small_send(), (in_slice, to_y)])
    small_sum = small_sum + small_got
    in_total = high_reps(add(in_slice, in_got))
    while small_moves:
        (small_got,), _ = ordered_round([small_send()])
        small_sum = small_sum + small_got
    to_both = pairs(lambda r, s: (r ^ 3, s))
    (in_away, by_core, by_y, by_both), _ = ordered_round(
        [(in_total, to_core)] + [(small_sum, perm) for perm in (to_core, to_y, to_both)]
    )
    small_sum = high_reps((small_sum + by_y) + (by_core + by_both))
    in_grad, out_grad = in_order(core, in_total, in_away, dq)
    small_total = lax.dynamic_slice_in_dim(
        small_sum, lax.axis_index("shard") * block, block, 1
    )
    return (
        *natural_outs,
        small_total[0],
        in_grad,
        small_total[2:],
        out_grad,
        small_total[1],
        gate_grad,
        up_grad,
        down_grad,
    )


def solution(mesh):
    in_specs = (
        P(("rep", "shard"), None),
        P("shard"),
        P("shard", None),
        P(None, "shard"),
        P(None, "shard"),
        P("shard"),
        P("shard", None),
        P("shard", None),
        P(None, "shard"),
        P(("rep", "shard"), None),
    )
    out_specs = (
        P(("rep", "shard"), None),
        P(("rep", "shard"), None),
        P("shard"),
        P("shard", None),
        P(None, "shard"),
        P(None, "shard"),
        P("shard"),
        P("shard", None),
        P("shard", None),
        P(None, "shard"),
    )
    body = functools.partial(shards, mesh.shape["rep"], mesh.shape["shard"])
    return jax.shard_map(body, mesh=mesh, in_specs=in_specs, out_specs=out_specs, check_vma=False)
```

```python
import functools

import jax
import jax.numpy as jnp
from jax import lax
from jax.experimental import pallas as pl
from jax.experimental.pallas import tpu as pltpu
from jax.sharding import PartitionSpec as P

SEQ = 512


EPSILON = 1e-05

AXES = ("rep", "shard")
PACK = 16


def plain_dot(left, right, kind=jnp.float32):
    return jnp.dot(left, right, preferred_element_type=jnp.float32).astype(kind)


def rows_dot(left, right):
    return lax.dot_general(
        left, right, (((1,), (1,)), ((), ())), preferred_element_type=jnp.float32
    )


def cols_dot(left, right):
    return lax.dot_general(
        left, right, (((0,), (0,)), ((), ())), preferred_element_type=jnp.float32
    ).astype(jnp.bfloat16)


def sigmoid(values):
    return 0.5 * jnp.tanh(0.5 * values) + 0.5


def kernel_call(body, steps, ins, outs):
    return pl.pallas_call(
        body,
        grid=(steps,),
        in_specs=[pl.BlockSpec(block, where) for _, block, where in ins],
        out_specs=[pl.BlockSpec(block, where) for _, _, block, where in outs],
        out_shape=[jax.ShapeDtypeStruct(shape, kind) for shape, kind, _, _ in outs],
        compiler_params=pltpu.CompilerParams(vmem_limit_bytes=56 * 2**20),
    )(*[v for v, _, _ in ins])


def same(n):
    return (0, 0)


def columns(n):
    return (0, n)


def rows(n):
    return (n, 0)


def gathered(piece_refs, weight_ref):
    extent = piece_refs[0].shape[0]
    for n, piece_ref in enumerate(piece_refs):
        weight_ref[n * extent : (n + 1) * extent, :] = piece_ref[...]


def feed(normed, pieces, tiles):
    count, depth = normed.shape
    extent = depth // len(pieces)
    pair = pieces[0].shape[1] // tiles
    tile = pair // 2

    def body(normed_ref, *refs):
        *piece_refs, pre_ref, hidden_ref, weight_ref = refs
        gathered(piece_refs, weight_ref)
        pre = jnp.dot(normed_ref[...], weight_ref[...], preferred_element_type=jnp.float32)
        pre_ref[...] = pre.astype(jnp.bfloat16)
        gate = pre[:, :tile]
        hidden_ref[...] = (gate * sigmoid(gate) * pre[:, tile:]).astype(jnp.bfloat16)

    return kernel_call(
        body,
        tiles,
        [(normed, (count, depth), same)] + [(v, (extent, pair), columns) for v in pieces],
        [
            ((count, tiles * pair), jnp.bfloat16, (count, pair), columns),
            ((count, tiles * tile), jnp.bfloat16, (count, tile), columns),
            ((depth, tiles * pair), jnp.bfloat16, (depth, pair), columns),
        ],
    )


def feed_and_down(normed, pieces, cot, half, at, tiles):
    count, depth = normed.shape
    extent = depth // len(pieces)
    pair = pieces[0].shape[1] // tiles
    tile = pair // 2
    n_pieces = len(pieces)
    operands = [] if half is None else [half]

    def body(normed_ref, cot_ref, *refs):
        piece_refs = refs[:n_pieces]
        pre_ref, hidden_ref, weight_ref, down_ref = refs[-4:]
        gathered(piece_refs, weight_ref)
        pre = jnp.dot(normed_ref[...], weight_ref[...], preferred_element_type=jnp.float32)
        pre_ref[...] = pre.astype(jnp.bfloat16)
        gate = pre[:, :tile]
        hidden_ref[...] = (gate * sigmoid(gate) * pre[:, tile:]).astype(jnp.bfloat16)
        down_ref[...] = cols_dot(cot_ref[...], hidden_ref[...])

    return pl.pallas_call(
        body,
        grid=(tiles,),
        in_specs=[pl.BlockSpec((count, depth), same)] * 2
        + [pl.BlockSpec((extent, pair), columns) for _ in pieces]
        + [pl.BlockSpec(memory_space=pl.ANY) for _ in operands],
        out_specs=[
            pl.BlockSpec((count, pair), columns),
            pl.BlockSpec((count, tile), columns),
            pl.BlockSpec((depth, pair), columns),
            pl.BlockSpec((depth, tile), lambda n: (0, n + at * tiles)),
        ],
        out_shape=[
            jax.ShapeDtypeStruct((count, tiles * pair), jnp.bfloat16),
            jax.ShapeDtypeStruct((count, tiles * tile), jnp.bfloat16),
            jax.ShapeDtypeStruct((depth, tiles * pair), jnp.bfloat16),
            jax.ShapeDtypeStruct((depth, 2 * tiles * tile), jnp.bfloat16),
        ],
        input_output_aliases={2 + n_pieces: 3} if operands else {},
        compiler_params=pltpu.CompilerParams(vmem_limit_bytes=56 * 2**20),
    )(normed, cot, *pieces, *operands)


def feed_back(cot, down_rows, pre, normed, tiles, first):
    count, depth = cot.shape
    pair = pre.shape[1] // tiles
    tile = pair // 2

    def body(cot_ref, down_ref, pre_ref, normed_ref, back_ref, local_ref):
        grad = rows_dot(cot_ref[...], down_ref[...])
        gate = pre_ref[:, :tile].astype(jnp.float32)
        up = pre_ref[:, tile:].astype(jnp.float32)
        sigma = sigmoid(gate)
        passed = grad * sigma
        back_ref[:, :tile] = (passed * up * (1.0 + gate * (1.0 - sigma))).astype(jnp.bfloat16)
        back_ref[:, tile:] = (passed * gate).astype(jnp.bfloat16)
        local_ref[...] = cols_dot(normed_ref[...], back_ref[...])

    return kernel_call(
        body,
        tiles,
        [
            (cot, (count, depth), same),
            (down_rows, (tile, depth), lambda n: (n + first, 0)),
            (pre, (count, pair), columns),
            (normed, (count, depth), same),
        ],
        [
            ((count, tiles * pair), jnp.bfloat16, (count, pair), columns),
            ((depth, tiles * pair), jnp.bfloat16, (depth, pair), columns),
        ],
    )


def down_local(cot, hidden, half, at):
    count, depth = cot.shape
    extent = hidden.shape[1]

    def body(cot_ref, hidden_ref, *refs):
        refs[-1][...] = cols_dot(cot_ref[...], hidden_ref[...])

    operands = [] if half is None else [half]
    return pl.pallas_call(
        body,
        grid=(1,),
        in_specs=[
            pl.BlockSpec((count, depth), same),
            pl.BlockSpec((count, extent), same),
        ]
        + [pl.BlockSpec(memory_space=pl.ANY) for _ in operands],
        out_specs=pl.BlockSpec((depth, extent), lambda n: (0, at)),
        out_shape=jax.ShapeDtypeStruct((depth, 2 * extent), jnp.bfloat16),
        input_output_aliases={2: 0} if operands else {},
        compiler_params=pltpu.CompilerParams(vmem_limit_bytes=56 * 2**20),
    )(cot, hidden, *operands)


def place_in_sequence(shape):
    return lax.rem(lax.broadcasted_iota(jnp.int32, shape, 0), SEQ)


def shifted(values, steps, at):
    inside = at >= steps if steps > 0 else at < SEQ + steps
    return jnp.where(inside, pltpu.roll(values, steps % values.shape[0], 0), 0.0)


def convolve(normed, pieces, taps, tiles):
    count, depth = normed.shape
    extent = depth // len(pieces)
    triple = pieces[0].shape[1] // tiles
    tile = triple // 3

    def body(normed_ref, taps_ref, *refs):
        *piece_refs, parts_ref, gated_ref, weight_ref = refs
        gathered(piece_refs, weight_ref)
        parts = jnp.dot(normed_ref[...], weight_ref[...], preferred_element_type=jnp.float32)
        parts_ref[...] = parts.astype(jnp.bfloat16)
        mixed = parts[:, :tile] * parts[:, 2 * tile :]
        at = place_in_sequence(mixed.shape)
        conv = (
            taps_ref[0:1, :] * shifted(mixed, 2, at)
            + taps_ref[1:2, :] * shifted(mixed, 1, at)
            + taps_ref[2:3, :] * mixed
        )
        gated_ref[...] = (parts[:, tile : 2 * tile] * conv).astype(jnp.bfloat16)

    return kernel_call(
        body,
        tiles,
        [(normed, (count, depth), same), (taps, (3, tile), columns)]
        + [(v, (extent, triple), columns) for v in pieces],
        [
            ((count, tiles * triple), jnp.bfloat16, (count, triple), columns),
            ((count, tiles * tile), jnp.bfloat16, (count, tile), columns),
            ((depth, tiles * triple), jnp.bfloat16, (depth, triple), columns),
        ],
    )


def convolve_back(branch_back, out_rows, parts, gated, taps, normed, tiles):
    count, depth = branch_back.shape
    triple = parts.shape[1] // tiles
    tile = triple // 3

    def body(
        branch_ref, out_ref, parts_ref, gated_ref, taps_ref, normed_ref,
        back_ref, local_ref, taps_local_ref,
    ):
        gated_grad = rows_dot(branch_ref[...], out_ref[...])
        b_part = parts_ref[:, :tile].astype(jnp.float32)
        c_part = parts_ref[:, tile : 2 * tile].astype(jnp.float32)
        x_part = parts_ref[:, 2 * tile :].astype(jnp.float32)
        mixed = b_part * x_part
        at = place_in_sequence(mixed.shape)
        before_1, before_2 = shifted(mixed, 1, at), shifted(mixed, 2, at)
        conv = (
            taps_ref[0:1, :] * before_2 + taps_ref[1:2, :] * before_1 + taps_ref[2:3, :] * mixed
        )
        conv_grad = gated_grad * c_part
        taps_local_ref[...] = jnp.concatenate(
            [
                jnp.sum(conv_grad * before_2, 0, keepdims=True),
                jnp.sum(conv_grad * before_1, 0, keepdims=True),
                jnp.sum(conv_grad * mixed, 0, keepdims=True),
            ],
            0,
        )
        mixed_grad = (
            taps_ref[2:3, :] * conv_grad
            + taps_ref[1:2, :] * shifted(conv_grad, -1, at)
            + taps_ref[0:1, :] * shifted(conv_grad, -2, at)
        )
        back_ref[:, :tile] = (mixed_grad * x_part).astype(jnp.bfloat16)
        back_ref[:, tile : 2 * tile] = (gated_grad * conv).astype(jnp.bfloat16)
        back_ref[:, 2 * tile :] = (mixed_grad * b_part).astype(jnp.bfloat16)
        local_ref[:, :triple] = cols_dot(normed_ref[...], back_ref[...])
        local_ref[:, triple:] = cols_dot(branch_ref[...], gated_ref[...])

    return kernel_call(
        body,
        tiles,
        [
            (branch_back, (count, depth), same),
            (out_rows, (tile, depth), rows),
            (parts, (count, triple), columns),
            (gated, (count, tile), columns),
            (taps, (3, tile), columns),
            (normed, (count, depth), same),
        ],
        [
            ((count, tiles * triple), jnp.bfloat16, (count, triple), columns),
            ((depth, tiles * 4 * tile), jnp.bfloat16, (depth, 4 * tile), columns),
            ((3, tiles * tile), jnp.float32, (3, tile), columns),
        ],
    )


def norm_back(backs, weights, values, inv_rms, gain, base, width):
    count, depth = values.shape
    total = len(backs)
    per = backs[0].shape[1] // width
    rows_at_once = min(128, count)

    def at(q):
        return lambda n: (0, jnp.clip(n - q * per, 0, per - 1))

    def body(*refs):
        back_refs, weight_refs = refs[:total], refs[total : 2 * total]
        values_ref, inv_ref, gain_ref, base_ref = refs[2 * total : 2 * total + 4]
        out_ref, gain_grad_ref, sum_ref = refs[-3:]
        n = pl.program_id(0)

        @pl.when(n == 0)
        def _():
            sum_ref[...] = rows_dot(back_refs[0][...], weight_refs[0][...])

        for q in range(total):

            @pl.when((n // per == q) & (n != 0))
            def _(q=q):
                sum_ref[...] += rows_dot(back_refs[q][...], weight_refs[q][...])

        @pl.when(n == total * per - 1)
        def _():
            def some_rows(at_chunk, gain_grad):
                here = pl.ds(pl.multiple_of(at_chunk * rows_at_once, rows_at_once), rows_at_once)
                grad = sum_ref[here, :]
                scaled = grad * gain_ref[...]
                held = values_ref[here, :].astype(jnp.float32)
                inv = inv_ref[here, :]
                mean = jnp.mean(scaled * held, -1, keepdims=True)
                made = inv * (scaled - held * (inv * inv * mean))
                out_ref[here, :] = (base_ref[here, :].astype(jnp.float32) + made).astype(
                    jnp.bfloat16
                )
                return gain_grad + jnp.sum(grad * held * inv, 0, keepdims=True)

            gain_grad_ref[...] = lax.fori_loop(
                0, count // rows_at_once, some_rows, jnp.zeros((1, depth), jnp.float32)
            )

    return pl.pallas_call(
        body,
        grid=(total * per,),
        in_specs=[pl.BlockSpec((count, width), at(q)) for q in range(total)]
        + [pl.BlockSpec((depth, width), at(q)) for q in range(total)]
        + [
            pl.BlockSpec((count, depth), same),
            pl.BlockSpec((count, 1), same),
            pl.BlockSpec((1, depth), same),
            pl.BlockSpec((count, depth), same),
        ],
        out_specs=[pl.BlockSpec((count, depth), same), pl.BlockSpec((1, depth), same)],
        out_shape=[
            jax.ShapeDtypeStruct((count, depth), jnp.bfloat16),
            jax.ShapeDtypeStruct((1, depth), jnp.float32),
        ],
        scratch_shapes=[pltpu.VMEM((count, depth), jnp.float32)],
        compiler_params=pltpu.CompilerParams(vmem_limit_bytes=56 * 2**20),
    )(*backs, *weights, values, inv_rms, gain[None, :], base)


def in_order(core, mine, other, quarter):
    block = mine.shape[0]

    def body(core_ref, mine_ref, other_ref, in_ref, out_ref):
        first = core_ref[0, 0] == 0
        halves = [
            jnp.where(first, mine_ref[...], other_ref[...]).astype(jnp.float32),
            jnp.where(first, other_ref[...], mine_ref[...]).astype(jnp.float32),
        ]
        for at in range(4):
            start = (at % 2) * 4 * quarter
            parts = halves[at // 2][:, start : start + 4 * quarter]
            for n in range(3):
                to = (4 * n + at) * quarter
                in_ref[:, to : to + quarter] = parts[:, n * quarter : (n + 1) * quarter]
            out_ref[at * quarter : (at + 1) * quarter, :] = parts[:, 3 * quarter :].T

    return pl.pallas_call(
        body,
        in_specs=[
            pl.BlockSpec(memory_space=pltpu.SMEM),
            pl.BlockSpec(memory_space=pltpu.VMEM),
            pl.BlockSpec(memory_space=pltpu.VMEM),
        ],
        out_specs=[pl.BlockSpec(memory_space=pltpu.VMEM)] * 2,
        out_shape=[
            jax.ShapeDtypeStruct((block, 12 * quarter), jnp.float32),
            jax.ShapeDtypeStruct((4 * quarter, block), jnp.float32),
        ],
        compiler_params=pltpu.CompilerParams(vmem_limit_bytes=56 * 2**20),
    )(core.astype(jnp.int32).reshape(1, 1), mine, other)


def down_in_order(core, mine, other):
    block, half = mine.shape

    def body(core_ref, mine_ref, other_ref, out_ref):
        first = core_ref[0, 0] == 0
        mine, other = mine_ref[...].astype(jnp.float32), other_ref[...].astype(jnp.float32)
        out_ref[:half, :] = jnp.where(first, mine, other).T
        out_ref[half:, :] = jnp.where(first, other, mine).T

    return pl.pallas_call(
        body,
        in_specs=[
            pl.BlockSpec(memory_space=pltpu.SMEM),
            pl.BlockSpec(memory_space=pltpu.VMEM),
            pl.BlockSpec(memory_space=pltpu.VMEM),
        ],
        out_specs=pl.BlockSpec(memory_space=pltpu.VMEM),
        out_shape=jax.ShapeDtypeStruct((2 * half, block), jnp.float32),
        compiler_params=pltpu.CompilerParams(vmem_limit_bytes=56 * 2**20),
    )(core.astype(jnp.int32).reshape(1, 1), mine, other)


def cycle_of(size):
    wide = size // 4
    walk = [(0, 0)]
    for row in range(4):
        cols = range(1, wide)
        walk += [(row, col) for col in (cols if row % 2 == 0 else reversed(cols))]
    walk += [(row, 0) for row in (3, 2, 1)]
    return [row * wide + col for row, col in walk]


def shards(
    reps,
    size,
    tokens,
    norm_gain_one,
    in_weight,
    conv_weight,
    out_weight,
    norm_gain_two,
    gate_weight,
    up_weight,
    down_weight,
    cotangent,
):
    bf16, f32 = jnp.bfloat16, jnp.float32
    width = tokens.shape[1]
    hidden_width = gate_weight.shape[1]
    block = width // size
    fq, dq = hidden_width // 4, width // 4
    tiles = 3 if fq % 384 == 0 else 1
    tile = fq // tiles
    ring = cycle_of(size)
    place = [ring.index(s) for s in range(size)]

    def pairs(move):
        return [
            (r * size + s, move(r, s)[0] * size + move(r, s)[1])
            for r in range(reps)
            for s in range(size)
        ]

    cw = pairs(lambda r, s: (r, ring[(place[s] + 1) % size]))
    ccw = pairs(lambda r, s: (r, ring[(place[s] - 1) % size]))
    to_core = pairs(lambda r, s: (r ^ 1, s))
    to_y = pairs(lambda r, s: (r ^ 2, s))

    def send(value, perm):
        return lax.ppermute(value, AXES, perm)

    rep = lax.axis_index("rep")
    core, ybit = rep % 2, (rep // 2) % 2
    at = jnp.asarray(place)[lax.axis_index("shard")]

    order = [0]
    for step in range(1, size // 2):
        order += [step, size - step]
    order += [size // 2]
    natural_block = jnp.asarray(ring)[(at - jnp.asarray(order)) % size]
    natural = (natural_block[:, None] * block + jnp.arange(block)[None, :]).reshape(-1)
    to_rel = (jnp.arange(width)[:, None] == natural[None, :]).astype(bf16)

    def quarter(i, j):
        return (core ^ i) * 2 + (ybit ^ j)

    quarters = ((0, 0), (0, 1), (1, 0), (1, 1))
    natural_feature = (
        jnp.stack([quarter(i, j) for i, j in quarters])[:, None] * dq + jnp.arange(dq)[None, :]
    ).reshape(-1)

    last = []

    def ordered_round(sends, work=None, args=()):
        leaves, tree = jax.tree.flatten(([v for v, _ in sends], tuple(args)))
        held = lax.optimization_barrier(tuple(leaves) + tuple(last))
        values, args = jax.tree.unflatten(tree, held[: len(leaves)])
        got = [send(v, perm) for v, (_, perm) in zip(values, sends)]
        made = work(*args) if work is not None else None
        last[:] = got + jax.tree.leaves(made)
        return got, made

    def cut_of(rows_of_piece):
        return rows_of_piece // 32 * 16

    class Gather:
        def __init__(self, piece, flip):
            self.got = {0: piece}
            self.halves = flip is None
            self.n_cw = size // 2 - (0 if flip is False else 1)
            self.n_ccw = size - 1 - self.n_cw - (1 if self.halves else 0)
            self.step = 0

        def sends(self):
            self.step += 1
            self.to = []
            out = []
            if self.halves and self.step == size // 2:
                before, after = self.got[self.step - 1], self.got[self.step + 1]
                cut = cut_of(before.shape[0])
                return [(before[:cut], cw), (after[cut:], ccw)]
            if self.step <= self.n_cw:
                out.append((self.got[self.step - 1], cw))
                self.to.append(self.step)
            if self.step <= self.n_ccw:
                out.append((self.got[(size - self.step + 1) % size], ccw))
                self.to.append(size - self.step)
            return out

        def take(self, got):
            if self.halves and self.step == size // 2:
                self.got[self.step] = jnp.concatenate(got, 0)
                return
            for b in self.to:
                self.got[b] = got.pop(0)

        def done(self):
            return self.step == size // 2

        def rows(self):
            return jnp.concatenate([self.got[b] for b in order], 0)

        def cols(self):
            return jnp.concatenate([self.got[b] for b in order], 1)

    class Scatter:
        def __init__(self, own, flip):
            self.own = own
            self.halves = flip is None
            self.n_cw = size // 2 - (0 if flip is False else 1)
            self.n_ccw = size - 1 - self.n_cw - (1 if self.halves else 0)
            self.step = size // 2 + 1
            self.up = self.down = None

        def sends(self):
            self.step -= 1
            out = []
            if self.halves and self.step == size // 2:
                far = total(*self.own(self.step))
                cut = cut_of(far.shape[0])
                return [(far[:cut], cw), (far[cut:], ccw)]
            if self.halves and self.step == size // 2 - 1:
                up, down = total(*self.own(size - self.step)), total(*self.own(self.step))
                cut = cut_of(up.shape[0])
                return [
                    (jnp.concatenate([total(up[:cut], self.up), up[cut:]], 0), cw),
                    (jnp.concatenate([down[:cut], total(down[cut:], self.down)], 0), ccw),
                ]
            if self.step <= self.n_cw:
                out.append((total(*self.own(size - self.step), self.up), cw))
            if self.step <= self.n_ccw:
                out.append((total(*self.own(self.step), self.down), ccw))
            return out

        def take(self, got):
            if self.halves and self.step == size // 2:
                self.up, self.down = got
                return
            if self.step <= self.n_cw:
                self.up = got.pop(0)
            if self.step <= self.n_ccw:
                self.down = got.pop(0)

        def done(self):
            return self.step == 1

        def result(self):
            return total(*self.own(0), self.up, self.down)

    def total(*values):
        values = [v for v in values if v is not None]
        if len(values) == 1:
            return values[0]
        return sum(v.astype(f32) for v in values).astype(bf16)

    def add(left, right):
        return total(left, right)

    def both_rounds(rings, others=(), work=None, args=()):
        sends = []
        counts = []
        for r in rings:
            mine = r.sends()
            counts.append(len(mine))
            sends += mine
        got, made = ordered_round(sends + list(others), work, args)
        for r, n in zip(rings, counts):
            r.take(got[:n])
            got = got[n:]
        return got, made

    def finish(*rings):
        while rings := [r for r in rings if not r.done()]:
            both_rounds(rings)

    def high_reps(value):
        step = 4
        while step < reps:
            other = send(value, pairs(lambda r, s: (r ^ step, s)))
            value = (value.astype(f32) + other.astype(f32)).astype(value.dtype)
            step *= 2
        return value

    def part(value, axis, i, j, extent):
        return lax.dynamic_slice_in_dim(value, quarter(i, j) * extent, extent, axis)

    def in_part(i, j):
        return part(in_weight.reshape(block, 3, width), 2, i, j, dq).reshape(block, 3 * dq)

    def gu_part(gate_weight, up_weight, i, j):
        both = [part(gate_weight, 1, i, j, fq), part(up_weight, 1, i, j, fq)]
        return jnp.concatenate(
            [w[:, t * tile : (t + 1) * tile] for t in range(tiles) for w in both], 1
        )

    def half_part(value):
        extent = value.shape[0] // 4
        return jnp.concatenate([part(value, 0, 0, j, extent) for j in range(2)], 0)

    small = jnp.concatenate([norm_gain_one, norm_gain_two, conv_weight.reshape(-1)])
    pack = jnp.pad(small[None, :], ((0, PACK - 1), (0, 6 * dq - small.shape[0])))
    in_ring = Gather(
        jnp.concatenate([jnp.concatenate([in_part(0, 0), in_part(0, 1)], 1), pack], 0), None
    )
    far_order = [b for b in order if b != 0]

    def far_send():
        b = far_order[len(far_pieces) - 1]
        return (gu_ring.got[b], to_y)

    def far_take(value):
        far_pieces[far_order[len(far_pieces) - 1]] = value

    def prepare(tokens, gate_weight, up_weight):
        tokens_rel = plain_dot(tokens, to_rel, bf16)
        values = tokens_rel.astype(f32)
        inv_one = lax.rsqrt(jnp.mean(values * values, -1, keepdims=True) + EPSILON)
        return tokens_rel, inv_one

    _, out_own = both_rounds([in_ring], (), half_part, (out_weight,))
    out_ring = Gather(out_own, True)
    _, (tokens_rel, inv_one) = both_rounds(
        [in_ring, out_ring], (), prepare, (tokens, gate_weight, up_weight)
    )
    _, gu_own = both_rounds(
        [in_ring, out_ring], (), lambda g, u: gu_part(g, u, 0, 0), (gate_weight, up_weight)
    )
    gu_ring = Gather(gu_own, True)
    _, far_own = both_rounds(
        [in_ring, out_ring], (), lambda g, u: gu_part(g, u, 0, 1), (gate_weight, up_weight)
    )
    far_pieces = {0: far_own}
    finish(in_ring)
    in_pieces = [in_ring.got[b] for b in order]
    packs = jnp.stack([v[block, : 5 * block] for v in in_pieces], 0).reshape(size, 5, block)
    gain_one_f = packs[:, 0].reshape(-1).astype(f32)
    gain_two_f = packs[:, 1].reshape(-1).astype(f32)
    to_feature = (natural[:, None] == natural_feature[None, :]).astype(bf16)
    taps = plain_dot(packs[:, 2:].transpose(1, 0, 2).reshape(3, width), to_feature)
    taps_h = (taps[:, : 2 * dq], taps[:, 2 * dq :])

    def project_first(tokens_rel, inv_one, gain, taps, *pieces):
        normed_one = (tokens_rel.astype(f32) * inv_one * gain).astype(bf16)
        return normed_one, convolve(normed_one, pieces, taps, 2)

    _, (normed_one, (parts_0, gated_0, in_half)) = both_rounds(
        [gu_ring, out_ring],
        (),
        project_first,
        (tokens_rel, inv_one, gain_one_f, taps_h[0], *in_pieces),
    )

    def prepare_more(cotangent, down_weight):
        return plain_dot(cotangent, to_rel, bf16), half_part(down_weight)

    finish(out_ring)
    out_half = out_ring.cols()
    (far, in_far, out_far), (cot, down_own) = both_rounds(
        [gu_ring],
        [far_send(), (in_half, to_core), (out_half, to_core)],
        prepare_more,
        (cotangent, down_weight),
    )
    far_take(far)
    down_ring = Gather(down_own, False)
    in_h = (in_half, in_far)

    def project_second(normed_one, weight, taps):
        return convolve(normed_one, [weight], taps, 2)[:2]

    (far,), (parts_1, gated_1) = both_rounds(
        [gu_ring], [far_send()], project_second, (normed_one, in_far, taps_h[1])
    )
    far_take(far)
    parts_h, gated_h = (parts_0, parts_1), (gated_0, gated_1)

    def mid(tokens_rel, g0, w0, g1, w1):
        middle = tokens_rel.astype(f32) + plain_dot(g0, w0) + plain_dot(g1, w1)
        inv_two = lax.rsqrt(jnp.mean(middle * middle, -1, keepdims=True) + EPSILON)
        return middle, inv_two, (middle * inv_two * gain_two_f).astype(bf16)

    gu_q = [None] * 4
    fed = [None] * 4

    def feed_tiles(normed, *pieces):
        return feed(normed, pieces, tiles)

    out_h = (out_half, out_far)
    (far,), (middle, inv_two, normed_two) = both_rounds(
        [gu_ring], [far_send()], mid, (tokens_rel, gated_0, out_half, gated_1, out_far)
    )
    far_take(far)
    finish(gu_ring)
    (far,), fed[0] = both_rounds(
        [down_ring], [far_send()], feed_tiles, (normed_two, *[gu_ring.got[b] for b in order])
    )
    far_take(far)
    gu_q[0] = fed[0][2]

    def down_first(cot, hidden):
        return down_local(cot, hidden, None, 0)

    def down_second(cot, hidden, half):
        return down_local(cot, hidden, half, 1)

    (far, gu_q[2]), down_0 = both_rounds(
        [down_ring], [far_send(), (gu_q[0], to_core)], down_first, (cot, fed[0][1])
    )
    far_take(far)

    def feed_both(normed, weight, cot, half, at):
        return feed_and_down(normed, [weight], cot, half, at, tiles)

    (far,), fed[2] = both_rounds(
        [down_ring],
        [far_send()],
        lambda *args: feed_both(*args, None, 0),
        (normed_two, gu_q[2], cot),
    )
    far_take(far)
    (far,), _ = both_rounds([down_ring], [far_send()])
    far_take(far)

    def row(value, b):
        n = order.index(b)
        return value[n * block : (n + 1) * block]

    finish(down_ring)
    while len(far_pieces) < size:
        (far,), _ = ordered_round([far_send()])
        far_take(far)
    down_half = down_ring.cols()
    (down_other,), fed[1] = ordered_round(
        [(down_half, to_core)], feed_tiles, (normed_two, *[far_pieces[b] for b in order])
    )
    gu_q[1] = fed[1][2]
    down_h = (down_half, down_other)
    (gu_q[3],), down_0 = ordered_round(
        [(gu_q[1], to_core)], down_second, (cot, fed[1][1], down_0)
    )

    _, fed[3] = ordered_round(
        [], lambda *args: feed_both(*args, 1), (normed_two, gu_q[3], cot, fed[2][3])
    )
    down_1 = fed[3][3]

    def feed_back_first(cot, down_rows, pre, normed):
        return feed_back(cot, down_rows, pre, normed, tiles, 0)

    def feed_back_second(cot, down_rows, pre, normed):
        return feed_back(cot, down_rows, pre, normed, tiles, tiles)

    def back_args(n):
        return (cot, down_h[n // 2], fed[n][0], normed_two)

    (down_far,), (back_3, local_3) = ordered_round(
        [(down_1, to_core)], feed_back_second, back_args(3)
    )
    (gu_far_1,), (back_1, local_1) = ordered_round(
        [(local_3, to_core)], feed_back_second, back_args(1)
    )
    down_s = Scatter(lambda b: (row(down_0, b), row(down_far, b)), False)
    y_order = [size // 2]
    for step in range(size // 2 - 1, 0, -1):
        y_order += [size - step, step]
    y_order += [0]
    y_got = {}

    def y_send():
        b = y_order[len(y_got)]
        return (total(row(local_1, b), row(gu_far_1, b)), to_y)

    def y_take(value):
        y_got[y_order[len(y_got)]] = value


    def sum_out(middle, h0, h1, w0, h2, h3, w1):
        return (
            middle
            + plain_dot(jnp.concatenate([h0, h1], 1), w0)
            + plain_dot(jnp.concatenate([h2, h3], 1), w1)
        ).astype(bf16)

    (away,), block_out = both_rounds(
        [down_s],
        [y_send()],
        sum_out,
        (middle, fed[0][1], fed[1][1], down_half, fed[2][1], fed[3][1], down_other),
    )
    y_take(away)
    (away,), (back_2, local_2) = both_rounds(
        [down_s], [y_send()], feed_back_first, back_args(2)
    )
    y_take(away)
    (away, gu_far_0), (back_0, local_0) = both_rounds(
        [down_s], [y_send(), (local_2, to_core)], feed_back_first, back_args(0)
    )
    y_take(away)
    gu_s = Scatter(lambda b: (row(local_0, b), row(gu_far_0, b), y_got[b]), False)

    def y_send_pair():
        at = min(order.index(y_order[len(y_got) + n]) for n in range(2))
        both = [v[at * block : (at + 2) * block] for v in (local_1, gu_far_1)]
        return (total(*both), to_y)

    def y_take_pair(value):
        at = min(order.index(y_order[len(y_got) + n]) for n in range(2))
        for n in range(2):
            y_got[order[at + n]] = value[n * block : (n + 1) * block]

    def mid_back(b0, w0, b1, w1, b2, w2, b3, w3, middle, inv_two, gain, cot):
        return norm_back(
            [b0, b1, b2, b3], [w0, w1, w2, w3], middle, inv_two, gain, cot, 2 * tile
        )

    mid_args = [v for n, back in enumerate((back_0, back_1, back_2, back_3)) for v in (back, gu_q[n])]
    (away,), (branch_back, gain_two_local) = both_rounds(
        [down_s, gu_s],
        [y_send_pair()],
        mid_back,
        (*mid_args, middle, inv_two, gain_two_f, cot),
    )
    y_take_pair(away)

    def conv_back_half(branch_back, out_rows, parts, gated, taps, normed_one):
        return convolve_back(branch_back, out_rows, parts, gated, taps, normed_one, 2)

    def conv_args(i):
        return (branch_back, out_h[i], parts_h[i], gated_h[i], taps_h[i], normed_one)

    (away,), (in_back_1, in_local_1, taps_local_1) = both_rounds(
        [gu_s], [y_send()], conv_back_half, conv_args(1)
    )
    y_take(away)
    (away, in_got), (in_back_0, in_local_0, taps_local_0) = both_rounds(
        [gu_s], [y_send(), (in_local_1, to_core)], conv_back_half, conv_args(0)
    )
    y_take(away)
    in_s = Scatter(lambda b: (row(in_local_0, b), row(in_got, b)), None)

    def swap(flag, first, second, axis):
        return jnp.where(
            flag == 0,
            jnp.concatenate([first, second], axis),
            jnp.concatenate([second, first], axis),
        )

    def y_ordered(value, axis):
        n = value.shape[axis] // 2
        return swap(
            ybit,
            lax.slice_in_dim(value, 0, n, axis=axis),
            lax.slice_in_dim(value, n, 2 * n, axis=axis),
            axis,
        )

    finish(down_s)
    down_slice = y_ordered(down_s.result(), 1)

    def first_back(b0, w0, b1, w1, tokens_rel, inv_one, gain, branch_back):
        return norm_back(
            [b0, b1], [w0, w1], tokens_rel, inv_one, gain, branch_back, 3 * dq
        )

    (away,), (tokens_grad, gain_one_local) = both_rounds(
        [gu_s, in_s],
        [y_send()],
        first_back,
        (in_back_0, in_h[0], in_back_1, in_h[1], tokens_rel, inv_one, gain_one_f, branch_back),
    )
    y_take(away)

    def to_natural(value):
        return rows_dot(value.astype(bf16), to_rel)

    def small_start(gain_one_local, gain_two_local, taps_0, taps_1):
        conv_natural = rows_dot(
            jnp.concatenate([taps_0, taps_1], 1).astype(bf16),
            (jnp.arange(width)[:, None] == natural_feature[None, :]).astype(bf16),
        )
        gains = to_natural(jnp.concatenate([gain_one_local, gain_two_local], 0))
        return jnp.concatenate([gains, conv_natural], 0)

    small_moves = []
    step = 1
    while step < size:
        small_moves.append(pairs(lambda r, s, step=step: (r, s ^ step)))
        step *= 2

    def small_send():
        return (small_sum, small_moves.pop(0))

    while len(y_got) < size:
        (away,), _ = ordered_round([y_send()])
        y_take(away)
    finish(gu_s)
    gu_slice = gu_s.result()

    gu_slice = high_reps(gu_slice)
    (gu_other,), (small_sum, tokens_natural) = both_rounds(
        [in_s],
        [(gu_slice, to_y)],
        lambda values, *small: (small_start(*small), to_natural(values).astype(bf16)),
        (tokens_grad, gain_one_local, gain_two_local, taps_local_0, taps_local_1),
    )
    gu_both = jnp.stack([gu_slice, gu_other], 0)
    (small_got, gu_far, down_got), block_natural = both_rounds(
        [in_s],
        [small_send(), (gu_both, to_core), (down_slice, to_y)],
        lambda v: to_natural(v).astype(bf16),
        (block_out,),
    )
    small_sum = small_sum + small_got

    def core_whole(mine, other, axis):
        return swap(core, mine, other, axis).astype(f32)

    def gu_out(gu_both, gu_far, start):
        def of(value):
            return jnp.concatenate(
                [value[:, (2 * t + start) * tile : (2 * t + start + 1) * tile] for t in range(tiles)], 1
            )

        own = swap(ybit, of(gu_both[0]), of(gu_both[1]), 1)
        far = swap(ybit, of(gu_far[0]), of(gu_far[1]), 1)
        return core_whole(own, far, 1)

    down_total = high_reps(add(down_slice, down_got))
    (small_got, down_away), (gate_grad, up_grad) = both_rounds(
        [in_s],
        [small_send(), (down_total, to_core)],
        lambda gu_both, gu_far: (gu_out(gu_both, gu_far, 0), gu_out(gu_both, gu_far, 1)),
        (gu_both, gu_far),
    )
    small_sum = small_sum + small_got
    finish(in_s)
    in_slice = y_ordered(in_s.result(), 1)
    (small_got, in_got), down_grad = ordered_round(
        [small_send(), (in_slice, to_y)],
        lambda mine, other: down_in_order(core, mine, other),
        (down_total, down_away),
    )
    small_sum = small_sum + small_got
    in_total = high_reps(add(in_slice, in_got))
    while small_moves:
        (small_got,), _ = ordered_round([small_send()])
        small_sum = small_sum + small_got
    to_both = pairs(lambda r, s: (r ^ 3, s))
    (in_away, by_core, by_y, by_both), _ = ordered_round(
        [(in_total, to_core)] + [(small_sum, perm) for perm in (to_core, to_y, to_both)]
    )
    small_sum = high_reps((small_sum + by_y) + (by_core + by_both))
    in_grad, out_grad = in_order(core, in_total, in_away, dq)
    small_total = lax.dynamic_slice_in_dim(
        small_sum, lax.axis_index("shard") * block, block, 1
    )
    return (
        block_natural,
        tokens_natural,
        small_total[0],
        in_grad,
        small_total[2:],
        out_grad,
        small_total[1],
        gate_grad,
        up_grad,
        down_grad,
    )


def solution(mesh):
    in_specs = (
        P(("rep", "shard"), None),
        P("shard"),
        P("shard", None),
        P(None, "shard"),
        P(None, "shard"),
        P("shard"),
        P("shard", None),
        P("shard", None),
        P(None, "shard"),
        P(("rep", "shard"), None),
    )
    out_specs = (
        P(("rep", "shard"), None),
        P(("rep", "shard"), None),
        P("shard"),
        P("shard", None),
        P(None, "shard"),
        P(None, "shard"),
        P("shard"),
        P("shard", None),
        P("shard", None),
        P(None, "shard"),
    )
    body = functools.partial(shards, mesh.shape["rep"], mesh.shape["shard"])
    return jax.shard_map(body, mesh=mesh, in_specs=in_specs, out_specs=out_specs, check_vma=False)
```

```python
import functools

import jax
import jax.numpy as jnp
from jax import lax
from jax.experimental import pallas as pl
from jax.experimental.pallas import tpu as pltpu
from jax.sharding import PartitionSpec as P

SEQ = 512


EPSILON = 1e-05

AXES = ("rep", "shard")
PACK = 16


def plain_dot(left, right, kind=jnp.float32):
    return jnp.dot(left, right, preferred_element_type=jnp.float32).astype(kind)


def rows_dot(left, right):
    return lax.dot_general(
        left, right, (((1,), (1,)), ((), ())), preferred_element_type=jnp.float32
    )


def cols_dot(left, right):
    return lax.dot_general(
        left, right, (((0,), (0,)), ((), ())), preferred_element_type=jnp.float32
    ).astype(jnp.bfloat16)


def sigmoid(values):
    return 0.5 * jnp.tanh(0.5 * values) + 0.5


def kernel_call(body, steps, ins, outs):
    return pl.pallas_call(
        body,
        grid=(steps,),
        in_specs=[pl.BlockSpec(block, where) for _, block, where in ins],
        out_specs=[pl.BlockSpec(block, where) for _, _, block, where in outs],
        out_shape=[jax.ShapeDtypeStruct(shape, kind) for shape, kind, _, _ in outs],
        compiler_params=pltpu.CompilerParams(vmem_limit_bytes=56 * 2**20),
    )(*[v for v, _, _ in ins])


def same(n):
    return (0, 0)


def columns(n):
    return (0, n)


def rows(n):
    return (n, 0)


def gathered(piece_refs, weight_ref):
    extent = piece_refs[0].shape[0]
    for n, piece_ref in enumerate(piece_refs):
        weight_ref[n * extent : (n + 1) * extent, :] = piece_ref[...]


def feed(normed, pieces, tiles):
    count, depth = normed.shape
    extent = depth // len(pieces)
    pair = pieces[0].shape[1] // tiles
    tile = pair // 2

    def body(normed_ref, *refs):
        *piece_refs, pre_ref, hidden_ref, weight_ref = refs
        gathered(piece_refs, weight_ref)
        pre = jnp.dot(normed_ref[...], weight_ref[...], preferred_element_type=jnp.float32)
        pre_ref[...] = pre.astype(jnp.bfloat16)
        gate = pre[:, :tile]
        hidden_ref[...] = (gate * sigmoid(gate) * pre[:, tile:]).astype(jnp.bfloat16)

    return kernel_call(
        body,
        tiles,
        [(normed, (count, depth), same)] + [(v, (extent, pair), columns) for v in pieces],
        [
            ((count, tiles * pair), jnp.bfloat16, (count, pair), columns),
            ((count, tiles * tile), jnp.bfloat16, (count, tile), columns),
            ((depth, tiles * pair), jnp.bfloat16, (depth, pair), columns),
        ],
    )


def feed_and_down(normed, pieces, cot, half, at, tiles):
    count, depth = normed.shape
    extent = depth // len(pieces)
    pair = pieces[0].shape[1] // tiles
    tile = pair // 2
    n_pieces = len(pieces)
    operands = [] if half is None else [half]

    def body(normed_ref, cot_ref, *refs):
        piece_refs = refs[:n_pieces]
        pre_ref, hidden_ref, weight_ref, down_ref = refs[-4:]
        gathered(piece_refs, weight_ref)
        pre = jnp.dot(normed_ref[...], weight_ref[...], preferred_element_type=jnp.float32)
        pre_ref[...] = pre.astype(jnp.bfloat16)
        gate = pre[:, :tile]
        hidden_ref[...] = (gate * sigmoid(gate) * pre[:, tile:]).astype(jnp.bfloat16)
        down_ref[...] = cols_dot(cot_ref[...], hidden_ref[...])

    return pl.pallas_call(
        body,
        grid=(tiles,),
        in_specs=[pl.BlockSpec((count, depth), same)] * 2
        + [pl.BlockSpec((extent, pair), columns) for _ in pieces]
        + [pl.BlockSpec(memory_space=pl.ANY) for _ in operands],
        out_specs=[
            pl.BlockSpec((count, pair), columns),
            pl.BlockSpec((count, tile), columns),
            pl.BlockSpec((depth, pair), columns),
            pl.BlockSpec((depth, tile), lambda n: (0, n + at * tiles)),
        ],
        out_shape=[
            jax.ShapeDtypeStruct((count, tiles * pair), jnp.bfloat16),
            jax.ShapeDtypeStruct((count, tiles * tile), jnp.bfloat16),
            jax.ShapeDtypeStruct((depth, tiles * pair), jnp.bfloat16),
            jax.ShapeDtypeStruct((depth, 2 * tiles * tile), jnp.bfloat16),
        ],
        input_output_aliases={2 + n_pieces: 3} if operands else {},
        compiler_params=pltpu.CompilerParams(vmem_limit_bytes=56 * 2**20),
    )(normed, cot, *pieces, *operands)


def feed_back(cot, down_rows, pre, normed, tiles, first):
    count, depth = cot.shape
    pair = pre.shape[1] // tiles
    tile = pair // 2

    def body(cot_ref, down_ref, pre_ref, normed_ref, back_ref, local_ref):
        grad = rows_dot(cot_ref[...], down_ref[...])
        gate = pre_ref[:, :tile].astype(jnp.float32)
        up = pre_ref[:, tile:].astype(jnp.float32)
        sigma = sigmoid(gate)
        passed = grad * sigma
        back_ref[:, :tile] = (passed * up * (1.0 + gate * (1.0 - sigma))).astype(jnp.bfloat16)
        back_ref[:, tile:] = (passed * gate).astype(jnp.bfloat16)
        local_ref[...] = cols_dot(normed_ref[...], back_ref[...])

    return kernel_call(
        body,
        tiles,
        [
            (cot, (count, depth), same),
            (down_rows, (tile, depth), lambda n: (n + first, 0)),
            (pre, (count, pair), columns),
            (normed, (count, depth), same),
        ],
        [
            ((count, tiles * pair), jnp.bfloat16, (count, pair), columns),
            ((depth, tiles * pair), jnp.bfloat16, (depth, pair), columns),
        ],
    )


def down_local(cot, hidden, half, at):
    count, depth = cot.shape
    extent = hidden.shape[1]

    def body(cot_ref, hidden_ref, *refs):
        refs[-1][...] = cols_dot(cot_ref[...], hidden_ref[...])

    operands = [] if half is None else [half]
    return pl.pallas_call(
        body,
        grid=(1,),
        in_specs=[
            pl.BlockSpec((count, depth), same),
            pl.BlockSpec((count, extent), same),
        ]
        + [pl.BlockSpec(memory_space=pl.ANY) for _ in operands],
        out_specs=pl.BlockSpec((depth, extent), lambda n: (0, at)),
        out_shape=jax.ShapeDtypeStruct((depth, 2 * extent), jnp.bfloat16),
        input_output_aliases={2: 0} if operands else {},
        compiler_params=pltpu.CompilerParams(vmem_limit_bytes=56 * 2**20),
    )(cot, hidden, *operands)


def place_in_sequence(shape):
    return lax.rem(lax.broadcasted_iota(jnp.int32, shape, 0), SEQ)


def shifted(values, steps, at):
    inside = at >= steps if steps > 0 else at < SEQ + steps
    return jnp.where(inside, pltpu.roll(values, steps % values.shape[0], 0), 0.0)


def convolve(normed, pieces, taps, tiles):
    count, depth = normed.shape
    extent = depth // len(pieces)
    triple = pieces[0].shape[1] // tiles
    tile = triple // 3

    def body(normed_ref, taps_ref, *refs):
        *piece_refs, parts_ref, gated_ref, weight_ref = refs
        gathered(piece_refs, weight_ref)
        parts = jnp.dot(normed_ref[...], weight_ref[...], preferred_element_type=jnp.float32)
        parts_ref[...] = parts.astype(jnp.bfloat16)
        mixed = parts[:, :tile] * parts[:, 2 * tile :]
        at = place_in_sequence(mixed.shape)
        conv = (
            taps_ref[0:1, :] * shifted(mixed, 2, at)
            + taps_ref[1:2, :] * shifted(mixed, 1, at)
            + taps_ref[2:3, :] * mixed
        )
        gated_ref[...] = (parts[:, tile : 2 * tile] * conv).astype(jnp.bfloat16)

    return kernel_call(
        body,
        tiles,
        [(normed, (count, depth), same), (taps, (3, tile), columns)]
        + [(v, (extent, triple), columns) for v in pieces],
        [
            ((count, tiles * triple), jnp.bfloat16, (count, triple), columns),
            ((count, tiles * tile), jnp.bfloat16, (count, tile), columns),
            ((depth, tiles * triple), jnp.bfloat16, (depth, triple), columns),
        ],
    )


def convolve_back(branch_back, out_rows, parts, gated, taps, normed, tiles):
    count, depth = branch_back.shape
    triple = parts.shape[1] // tiles
    tile = triple // 3

    def body(
        branch_ref, out_ref, parts_ref, gated_ref, taps_ref, normed_ref,
        back_ref, local_ref, taps_local_ref,
    ):
        gated_grad = rows_dot(branch_ref[...], out_ref[...])
        b_part = parts_ref[:, :tile].astype(jnp.float32)
        c_part = parts_ref[:, tile : 2 * tile].astype(jnp.float32)
        x_part = parts_ref[:, 2 * tile :].astype(jnp.float32)
        mixed = b_part * x_part
        at = place_in_sequence(mixed.shape)
        before_1, before_2 = shifted(mixed, 1, at), shifted(mixed, 2, at)
        conv = (
            taps_ref[0:1, :] * before_2 + taps_ref[1:2, :] * before_1 + taps_ref[2:3, :] * mixed
        )
        conv_grad = gated_grad * c_part
        taps_local_ref[...] = jnp.concatenate(
            [
                jnp.sum(conv_grad * before_2, 0, keepdims=True),
                jnp.sum(conv_grad * before_1, 0, keepdims=True),
                jnp.sum(conv_grad * mixed, 0, keepdims=True),
            ],
            0,
        )
        mixed_grad = (
            taps_ref[2:3, :] * conv_grad
            + taps_ref[1:2, :] * shifted(conv_grad, -1, at)
            + taps_ref[0:1, :] * shifted(conv_grad, -2, at)
        )
        back_ref[:, :tile] = (mixed_grad * x_part).astype(jnp.bfloat16)
        back_ref[:, tile : 2 * tile] = (gated_grad * conv).astype(jnp.bfloat16)
        back_ref[:, 2 * tile :] = (mixed_grad * b_part).astype(jnp.bfloat16)
        local_ref[:, :triple] = cols_dot(normed_ref[...], back_ref[...])
        local_ref[:, triple:] = cols_dot(branch_ref[...], gated_ref[...])

    return kernel_call(
        body,
        tiles,
        [
            (branch_back, (count, depth), same),
            (out_rows, (tile, depth), rows),
            (parts, (count, triple), columns),
            (gated, (count, tile), columns),
            (taps, (3, tile), columns),
            (normed, (count, depth), same),
        ],
        [
            ((count, tiles * triple), jnp.bfloat16, (count, triple), columns),
            ((depth, tiles * 4 * tile), jnp.bfloat16, (depth, 4 * tile), columns),
            ((3, tiles * tile), jnp.float32, (3, tile), columns),
        ],
    )


def norm_back(backs, weights, values, inv_rms, gain, base, width):
    count, depth = values.shape
    total = len(backs)
    per = backs[0].shape[1] // width
    rows_at_once = min(128, count)

    def at(q):
        return lambda n: (0, jnp.clip(n - q * per, 0, per - 1))

    def body(*refs):
        back_refs, weight_refs = refs[:total], refs[total : 2 * total]
        values_ref, inv_ref, gain_ref, base_ref = refs[2 * total : 2 * total + 4]
        out_ref, gain_grad_ref, sum_ref = refs[-3:]
        n = pl.program_id(0)

        @pl.when(n == 0)
        def _():
            sum_ref[...] = rows_dot(back_refs[0][...], weight_refs[0][...])

        for q in range(total):

            @pl.when((n // per == q) & (n != 0))
            def _(q=q):
                sum_ref[...] += rows_dot(back_refs[q][...], weight_refs[q][...])

        @pl.when(n == total * per - 1)
        def _():
            def some_rows(at_chunk, gain_grad):
                here = pl.ds(pl.multiple_of(at_chunk * rows_at_once, rows_at_once), rows_at_once)
                grad = sum_ref[here, :]
                scaled = grad * gain_ref[...]
                held = values_ref[here, :].astype(jnp.float32)
                inv = inv_ref[here, :]
                mean = jnp.mean(scaled * held, -1, keepdims=True)
                made = inv * (scaled - held * (inv * inv * mean))
                out_ref[here, :] = (base_ref[here, :].astype(jnp.float32) + made).astype(
                    jnp.bfloat16
                )
                return gain_grad + jnp.sum(grad * held * inv, 0, keepdims=True)

            gain_grad_ref[...] = lax.fori_loop(
                0, count // rows_at_once, some_rows, jnp.zeros((1, depth), jnp.float32)
            )

    return pl.pallas_call(
        body,
        grid=(total * per,),
        in_specs=[pl.BlockSpec((count, width), at(q)) for q in range(total)]
        + [pl.BlockSpec((depth, width), at(q)) for q in range(total)]
        + [
            pl.BlockSpec((count, depth), same),
            pl.BlockSpec((count, 1), same),
            pl.BlockSpec((1, depth), same),
            pl.BlockSpec((count, depth), same),
        ],
        out_specs=[pl.BlockSpec((count, depth), same), pl.BlockSpec((1, depth), same)],
        out_shape=[
            jax.ShapeDtypeStruct((count, depth), jnp.bfloat16),
            jax.ShapeDtypeStruct((1, depth), jnp.float32),
        ],
        scratch_shapes=[pltpu.VMEM((count, depth), jnp.float32)],
        compiler_params=pltpu.CompilerParams(vmem_limit_bytes=56 * 2**20),
    )(*backs, *weights, values, inv_rms, gain[None, :], base)


def in_order(core, mine, other, quarter):
    block = mine.shape[0]

    def body(core_ref, mine_ref, other_ref, in_ref, out_ref):
        first = core_ref[0, 0] == 0
        halves = [
            jnp.where(first, mine_ref[...], other_ref[...]).astype(jnp.float32),
            jnp.where(first, other_ref[...], mine_ref[...]).astype(jnp.float32),
        ]
        for at in range(4):
            start = (at % 2) * 4 * quarter
            parts = halves[at // 2][:, start : start + 4 * quarter]
            for n in range(3):
                to = (4 * n + at) * quarter
                in_ref[:, to : to + quarter] = parts[:, n * quarter : (n + 1) * quarter]
            out_ref[at * quarter : (at + 1) * quarter, :] = parts[:, 3 * quarter :].T

    return pl.pallas_call(
        body,
        in_specs=[
            pl.BlockSpec(memory_space=pltpu.SMEM),
            pl.BlockSpec(memory_space=pltpu.VMEM),
            pl.BlockSpec(memory_space=pltpu.VMEM),
        ],
        out_specs=[pl.BlockSpec(memory_space=pltpu.VMEM)] * 2,
        out_shape=[
            jax.ShapeDtypeStruct((block, 12 * quarter), jnp.float32),
            jax.ShapeDtypeStruct((4 * quarter, block), jnp.float32),
        ],
        compiler_params=pltpu.CompilerParams(vmem_limit_bytes=56 * 2**20),
    )(core.astype(jnp.int32).reshape(1, 1), mine, other)


def down_in_order(core, mine, other):
    block, half = mine.shape

    def body(core_ref, mine_ref, other_ref, out_ref):
        first = core_ref[0, 0] == 0
        mine, other = mine_ref[...].astype(jnp.float32), other_ref[...].astype(jnp.float32)
        out_ref[:half, :] = jnp.where(first, mine, other).T
        out_ref[half:, :] = jnp.where(first, other, mine).T

    return pl.pallas_call(
        body,
        in_specs=[
            pl.BlockSpec(memory_space=pltpu.SMEM),
            pl.BlockSpec(memory_space=pltpu.VMEM),
            pl.BlockSpec(memory_space=pltpu.VMEM),
        ],
        out_specs=pl.BlockSpec(memory_space=pltpu.VMEM),
        out_shape=jax.ShapeDtypeStruct((2 * half, block), jnp.float32),
        compiler_params=pltpu.CompilerParams(vmem_limit_bytes=56 * 2**20),
    )(core.astype(jnp.int32).reshape(1, 1), mine, other)


def cycle_of(size):
    wide = size // 4
    walk = [(0, 0)]
    for row in range(4):
        cols = range(1, wide)
        walk += [(row, col) for col in (cols if row % 2 == 0 else reversed(cols))]
    walk += [(row, 0) for row in (3, 2, 1)]
    return [row * wide + col for row, col in walk]


def shards(
    reps,
    size,
    tokens,
    norm_gain_one,
    in_weight,
    conv_weight,
    out_weight,
    norm_gain_two,
    gate_weight,
    up_weight,
    down_weight,
    cotangent,
):
    bf16, f32 = jnp.bfloat16, jnp.float32
    width = tokens.shape[1]
    hidden_width = gate_weight.shape[1]
    block = width // size
    fq, dq = hidden_width // 4, width // 4
    tiles = 3 if fq % 384 == 0 else 1
    tile = fq // tiles
    ring = cycle_of(size)
    place = [ring.index(s) for s in range(size)]

    def pairs(move):
        return [
            (r * size + s, move(r, s)[0] * size + move(r, s)[1])
            for r in range(reps)
            for s in range(size)
        ]

    cw = pairs(lambda r, s: (r, ring[(place[s] + 1) % size]))
    ccw = pairs(lambda r, s: (r, ring[(place[s] - 1) % size]))
    to_core = pairs(lambda r, s: (r ^ 1, s))
    to_y = pairs(lambda r, s: (r ^ 2, s))

    def send(value, perm):
        return lax.ppermute(value, AXES, perm)

    rep = lax.axis_index("rep")
    core, ybit = rep % 2, (rep // 2) % 2
    at = jnp.asarray(place)[lax.axis_index("shard")]

    order = [0]
    for step in range(1, size // 2):
        order += [step, size - step]
    order += [size // 2]
    natural_block = jnp.asarray(ring)[(at - jnp.asarray(order)) % size]
    natural = (natural_block[:, None] * block + jnp.arange(block)[None, :]).reshape(-1)
    to_rel = (jnp.arange(width)[:, None] == natural[None, :]).astype(bf16)

    def quarter(i, j):
        return (core ^ i) * 2 + (ybit ^ j)

    quarters = ((0, 0), (0, 1), (1, 0), (1, 1))
    natural_feature = (
        jnp.stack([quarter(i, j) for i, j in quarters])[:, None] * dq + jnp.arange(dq)[None, :]
    ).reshape(-1)

    last = []

    def ordered_round(sends, work=None, args=()):
        leaves, tree = jax.tree.flatten(([v for v, _ in sends], tuple(args)))
        held = lax.optimization_barrier(tuple(leaves) + tuple(last))
        values, args = jax.tree.unflatten(tree, held[: len(leaves)])
        got = [send(v, perm) for v, (_, perm) in zip(values, sends)]
        made = work(*args) if work is not None else None
        last[:] = got + jax.tree.leaves(made)
        return got, made

    def cut_of(rows_of_piece):
        return rows_of_piece // 32 * 16

    class Gather:
        def __init__(self, piece, flip):
            self.got = {0: piece}
            self.halves = flip is None
            self.n_cw = size // 2 - (0 if flip is False else 1)
            self.n_ccw = size - 1 - self.n_cw - (1 if self.halves else 0)
            self.step = 0

        def sends(self):
            self.step += 1
            self.to = []
            out = []
            if self.halves and self.step == size // 2:
                before, after = self.got[self.step - 1], self.got[self.step + 1]
                cut = cut_of(before.shape[0])
                return [(before[:cut], cw), (after[cut:], ccw)]
            if self.step <= self.n_cw:
                out.append((self.got[self.step - 1], cw))
                self.to.append(self.step)
            if self.step <= self.n_ccw:
                out.append((self.got[(size - self.step + 1) % size], ccw))
                self.to.append(size - self.step)
            return out

        def take(self, got):
            if self.halves and self.step == size // 2:
                self.got[self.step] = jnp.concatenate(got, 0)
                return
            for b in self.to:
                self.got[b] = got.pop(0)

        def done(self):
            return self.step == size // 2

        def rows(self):
            return jnp.concatenate([self.got[b] for b in order], 0)

        def cols(self):
            return jnp.concatenate([self.got[b] for b in order], 1)

    class Scatter:
        def __init__(self, own, flip):
            self.own = own
            self.halves = flip is None
            self.n_cw = size // 2 - (0 if flip is False else 1)
            self.n_ccw = size - 1 - self.n_cw - (1 if self.halves else 0)
            self.step = size // 2 + 1
            self.up = self.down = None

        def sends(self):
            self.step -= 1
            out = []
            if self.halves and self.step == size // 2:
                far = total(*self.own(self.step))
                cut = cut_of(far.shape[0])
                return [(far[:cut], cw), (far[cut:], ccw)]
            if self.halves and self.step == size // 2 - 1:
                up, down = total(*self.own(size - self.step)), total(*self.own(self.step))
                cut = cut_of(up.shape[0])
                return [
                    (jnp.concatenate([total(up[:cut], self.up), up[cut:]], 0), cw),
                    (jnp.concatenate([down[:cut], total(down[cut:], self.down)], 0), ccw),
                ]
            if self.step <= self.n_cw:
                out.append((total(*self.own(size - self.step), self.up), cw))
            if self.step <= self.n_ccw:
                out.append((total(*self.own(self.step), self.down), ccw))
            return out

        def take(self, got):
            if self.halves and self.step == size // 2:
                self.up, self.down = got
                return
            if self.step <= self.n_cw:
                self.up = got.pop(0)
            if self.step <= self.n_ccw:
                self.down = got.pop(0)

        def done(self):
            return self.step == 1

        def result(self):
            return total(*self.own(0), self.up, self.down)

    def total(*values):
        values = [v for v in values if v is not None]
        if len(values) == 1:
            return values[0]
        return sum(v.astype(f32) for v in values).astype(bf16)

    def add(left, right):
        return total(left, right)

    def both_rounds(rings, others=(), work=None, args=()):
        sends = []
        counts = []
        for r in rings:
            mine = r.sends()
            counts.append(len(mine))
            sends += mine
        got, made = ordered_round(sends + list(others), work, args)
        for r, n in zip(rings, counts):
            r.take(got[:n])
            got = got[n:]
        return got, made

    def finish(*rings):
        while rings := [r for r in rings if not r.done()]:
            both_rounds(rings)

    def high_reps(value):
        step = 4
        while step < reps:
            other = send(value, pairs(lambda r, s: (r ^ step, s)))
            value = (value.astype(f32) + other.astype(f32)).astype(value.dtype)
            step *= 2
        return value

    def part(value, axis, i, j, extent):
        return lax.dynamic_slice_in_dim(value, quarter(i, j) * extent, extent, axis)

    def in_part(i, j):
        return part(in_weight.reshape(block, 3, width), 2, i, j, dq).reshape(block, 3 * dq)

    def gu_part(gate_weight, up_weight, i, j):
        both = [part(gate_weight, 1, i, j, fq), part(up_weight, 1, i, j, fq)]
        return jnp.concatenate(
            [w[:, t * tile : (t + 1) * tile] for t in range(tiles) for w in both], 1
        )

    def half_part(value):
        extent = value.shape[0] // 4
        return jnp.concatenate([part(value, 0, 0, j, extent) for j in range(2)], 0)

    small = jnp.concatenate([norm_gain_one, norm_gain_two, conv_weight.reshape(-1)])
    pack = jnp.pad(small[None, :], ((0, PACK - 1), (0, 6 * dq - small.shape[0])))
    in_ring = Gather(
        jnp.concatenate([jnp.concatenate([in_part(0, 0), in_part(0, 1)], 1), pack], 0), None
    )
    far_order = [b for b in order if b != 0]

    def far_send():
        b = far_order[len(far_pieces) - 1]
        return (gu_ring.got[b], to_y)

    def far_take(value):
        far_pieces[far_order[len(far_pieces) - 1]] = value

    def prepare(tokens, gate_weight, up_weight):
        tokens_rel = plain_dot(tokens, to_rel, bf16)
        values = tokens_rel.astype(f32)
        inv_one = lax.rsqrt(jnp.mean(values * values, -1, keepdims=True) + EPSILON)
        return tokens_rel, inv_one

    _, out_own = both_rounds([in_ring], (), half_part, (out_weight,))
    out_ring = Gather(out_own, True)
    _, (tokens_rel, inv_one) = both_rounds(
        [in_ring, out_ring], (), prepare, (tokens, gate_weight, up_weight)
    )
    _, gu_own = both_rounds(
        [in_ring, out_ring], (), lambda g, u: gu_part(g, u, 0, 0), (gate_weight, up_weight)
    )
    gu_ring = Gather(gu_own, True)
    _, far_own = both_rounds(
        [in_ring, out_ring], (), lambda g, u: gu_part(g, u, 0, 1), (gate_weight, up_weight)
    )
    far_pieces = {0: far_own}
    finish(in_ring)
    in_pieces = [in_ring.got[b] for b in order]
    packs = jnp.stack([v[block, : 5 * block] for v in in_pieces], 0).reshape(size, 5, block)
    gain_one_f = packs[:, 0].reshape(-1).astype(f32)
    gain_two_f = packs[:, 1].reshape(-1).astype(f32)
    to_feature = (natural[:, None] == natural_feature[None, :]).astype(bf16)
    taps = plain_dot(packs[:, 2:].transpose(1, 0, 2).reshape(3, width), to_feature)
    taps_h = (taps[:, : 2 * dq], taps[:, 2 * dq :])

    def project_first(tokens_rel, inv_one, gain, taps, *pieces):
        normed_one = (tokens_rel.astype(f32) * inv_one * gain).astype(bf16)
        return normed_one, convolve(normed_one, pieces, taps, 2)

    _, (normed_one, (parts_0, gated_0, in_half)) = both_rounds(
        [gu_ring, out_ring],
        (),
        project_first,
        (tokens_rel, inv_one, gain_one_f, taps_h[0], *in_pieces),
    )

    def prepare_more(cotangent, down_weight):
        return plain_dot(cotangent, to_rel, bf16), half_part(down_weight)

    finish(out_ring)
    out_half = out_ring.cols()
    (far, in_far, out_far), (cot, down_own) = both_rounds(
        [gu_ring],
        [far_send(), (in_half, to_core), (out_half, to_core)],
        prepare_more,
        (cotangent, down_weight),
    )
    far_take(far)
    down_ring = Gather(down_own, False)
    in_h = (in_half, in_far)

    def project_second(normed_one, weight, taps):
        return convolve(normed_one, [weight], taps, 2)[:2]

    (far,), (parts_1, gated_1) = both_rounds(
        [gu_ring], [far_send()], project_second, (normed_one, in_far, taps_h[1])
    )
    far_take(far)
    parts_h, gated_h = (parts_0, parts_1), (gated_0, gated_1)

    def mid(tokens_rel, g0, w0, g1, w1):
        middle = tokens_rel.astype(f32) + plain_dot(g0, w0) + plain_dot(g1, w1)
        inv_two = lax.rsqrt(jnp.mean(middle * middle, -1, keepdims=True) + EPSILON)
        return middle, inv_two, (middle * inv_two * gain_two_f).astype(bf16)

    gu_q = [None] * 4
    fed = [None] * 4

    def feed_tiles(normed, *pieces):
        return feed(normed, pieces, tiles)

    out_h = (out_half, out_far)
    (far,), (middle, inv_two, normed_two) = both_rounds(
        [gu_ring], [far_send()], mid, (tokens_rel, gated_0, out_half, gated_1, out_far)
    )
    far_take(far)
    finish(gu_ring)
    (far,), fed[0] = both_rounds(
        [down_ring], [far_send()], feed_tiles, (normed_two, *[gu_ring.got[b] for b in order])
    )
    far_take(far)
    gu_q[0] = fed[0][2]

    def down_first(cot, hidden):
        return down_local(cot, hidden, None, 0)

    def down_second(cot, hidden, half):
        return down_local(cot, hidden, half, 1)

    (far, gu_q[2]), down_0 = both_rounds(
        [down_ring], [far_send(), (gu_q[0], to_core)], down_first, (cot, fed[0][1])
    )
    far_take(far)

    def feed_both(normed, weight, cot, half, at):
        return feed_and_down(normed, [weight], cot, half, at, tiles)

    (far,), fed[2] = both_rounds(
        [down_ring],
        [far_send()],
        lambda *args: feed_both(*args, None, 0),
        (normed_two, gu_q[2], cot),
    )
    far_take(far)
    (far,), _ = both_rounds([down_ring], [far_send()])
    far_take(far)

    def row(value, b):
        n = order.index(b)
        return value[n * block : (n + 1) * block]

    finish(down_ring)
    while len(far_pieces) < size:
        (far,), _ = ordered_round([far_send()])
        far_take(far)
    down_half = down_ring.cols()
    (down_other,), fed[1] = ordered_round(
        [(down_half, to_core)], feed_tiles, (normed_two, *[far_pieces[b] for b in order])
    )
    gu_q[1] = fed[1][2]
    down_h = (down_half, down_other)
    (gu_q[3],), down_0 = ordered_round(
        [(gu_q[1], to_core)], down_second, (cot, fed[1][1], down_0)
    )

    _, fed[3] = ordered_round(
        [], lambda *args: feed_both(*args, 1), (normed_two, gu_q[3], cot, fed[2][3])
    )
    down_1 = fed[3][3]

    def feed_back_first(cot, down_rows, pre, normed):
        return feed_back(cot, down_rows, pre, normed, tiles, 0)

    def feed_back_second(cot, down_rows, pre, normed):
        return feed_back(cot, down_rows, pre, normed, tiles, tiles)

    def back_args(n):
        return (cot, down_h[n // 2], fed[n][0], normed_two)

    (down_far,), (back_3, local_3) = ordered_round(
        [(down_1, to_core)], feed_back_second, back_args(3)
    )
    (gu_far_1,), (back_1, local_1) = ordered_round(
        [(local_3, to_core)], feed_back_second, back_args(1)
    )
    down_s = Scatter(lambda b: (row(down_0, b), row(down_far, b)), False)
    y_order = [size // 2]
    for step in range(size // 2 - 1, 0, -1):
        y_order += [size - step, step]
    y_order += [0]
    y_got = {}

    def y_send():
        b = y_order[len(y_got)]
        return (total(row(local_1, b), row(gu_far_1, b)), to_y)

    def y_take(value):
        y_got[y_order[len(y_got)]] = value


    def sum_out(middle, h0, h1, w0, h2, h3, w1):
        return (
            middle
            + plain_dot(jnp.concatenate([h0, h1], 1), w0)
            + plain_dot(jnp.concatenate([h2, h3], 1), w1)
        ).astype(bf16)

    (away,), block_out = both_rounds(
        [down_s],
        [y_send()],
        sum_out,
        (middle, fed[0][1], fed[1][1], down_half, fed[2][1], fed[3][1], down_other),
    )
    y_take(away)
    (away,), (back_2, local_2) = both_rounds(
        [down_s], [y_send()], feed_back_first, back_args(2)
    )
    y_take(away)
    (away, gu_far_0), (back_0, local_0) = both_rounds(
        [down_s], [y_send(), (local_2, to_core)], feed_back_first, back_args(0)
    )
    y_take(away)
    gu_s = Scatter(lambda b: (row(local_0, b), row(gu_far_0, b), y_got[b]), False)

    def y_send_pair():
        at = min(order.index(y_order[len(y_got) + n]) for n in range(2))
        both = [v[at * block : (at + 2) * block] for v in (local_1, gu_far_1)]
        return (total(*both), to_y)

    def y_take_pair(value):
        at = min(order.index(y_order[len(y_got) + n]) for n in range(2))
        for n in range(2):
            y_got[order[at + n]] = value[n * block : (n + 1) * block]

    def mid_back(b0, w0, b1, w1, b2, w2, b3, w3, middle, inv_two, gain, cot):
        return norm_back(
            [b0, b1, b2, b3], [w0, w1, w2, w3], middle, inv_two, gain, cot, 2 * tile
        )

    mid_args = [v for n, back in enumerate((back_0, back_1, back_2, back_3)) for v in (back, gu_q[n])]
    (away,), (branch_back, gain_two_local) = both_rounds(
        [down_s, gu_s],
        [y_send_pair()],
        mid_back,
        (*mid_args, middle, inv_two, gain_two_f, cot),
    )
    y_take_pair(away)

    def conv_back_half(branch_back, out_rows, parts, gated, taps, normed_one):
        return convolve_back(branch_back, out_rows, parts, gated, taps, normed_one, 2)

    def conv_args(i):
        return (branch_back, out_h[i], parts_h[i], gated_h[i], taps_h[i], normed_one)

    (away,), (in_back_1, in_local_1, taps_local_1) = both_rounds(
        [gu_s], [y_send()], conv_back_half, conv_args(1)
    )
    y_take(away)
    (away, in_got), (in_back_0, in_local_0, taps_local_0) = both_rounds(
        [gu_s], [y_send(), (in_local_1, to_core)], conv_back_half, conv_args(0)
    )
    y_take(away)
    in_s = Scatter(lambda b: (row(in_local_0, b), row(in_got, b)), None)

    def swap(flag, first, second, axis):
        return jnp.where(
            flag == 0,
            jnp.concatenate([first, second], axis),
            jnp.concatenate([second, first], axis),
        )

    def y_ordered(value, axis):
        n = value.shape[axis] // 2
        return swap(
            ybit,
            lax.slice_in_dim(value, 0, n, axis=axis),
            lax.slice_in_dim(value, n, 2 * n, axis=axis),
            axis,
        )

    finish(down_s)
    down_slice = y_ordered(down_s.result(), 1)

    def first_back(b0, w0, b1, w1, tokens_rel, inv_one, gain, branch_back):
        return norm_back(
            [b0, b1], [w0, w1], tokens_rel, inv_one, gain, branch_back, 3 * dq
        )

    (away,), (tokens_grad, gain_one_local) = both_rounds(
        [gu_s, in_s],
        [y_send()],
        first_back,
        (in_back_0, in_h[0], in_back_1, in_h[1], tokens_rel, inv_one, gain_one_f, branch_back),
    )
    y_take(away)

    def to_natural(value):
        return rows_dot(value.astype(bf16), to_rel)

    def small_start(gain_one_local, gain_two_local, taps_0, taps_1):
        conv_natural = rows_dot(
            jnp.concatenate([taps_0, taps_1], 1).astype(bf16),
            (jnp.arange(width)[:, None] == natural_feature[None, :]).astype(bf16),
        )
        gains = to_natural(jnp.concatenate([gain_one_local, gain_two_local], 0))
        return jnp.concatenate([gains, conv_natural], 0)

    def over_shard(*bits):
        return [pairs(lambda r, s, bit=bit: (r, s ^ bit)) for bit in bits]

    small_moves = [over_shard(1), over_shard(2, 4, 6)]
    step = 8
    while step < size:
        small_moves.append(over_shard(step))
        step *= 2
    small_moves.append([to_core, to_y, pairs(lambda r, s: (r ^ 3, s))])

    def small_sends():
        return [(small_sum, perm) for perm in small_moves.pop(0)]

    def small_added(got):
        if len(got) == 1:
            return small_sum + got[0]
        return (small_sum + got[0]) + (got[1] + got[2])

    while len(y_got) < size:
        (away,), _ = ordered_round([y_send()])
        y_take(away)
    finish(gu_s)
    gu_slice = gu_s.result()

    gu_slice = high_reps(gu_slice)
    (gu_other,), (small_sum, tokens_natural) = both_rounds(
        [in_s],
        [(gu_slice, to_y)],
        lambda values, *small: (small_start(*small), to_natural(values).astype(bf16)),
        (tokens_grad, gain_one_local, gain_two_local, taps_local_0, taps_local_1),
    )
    gu_both = jnp.stack([gu_slice, gu_other], 0)
    (small_got, gu_far, down_got), block_natural = both_rounds(
        [in_s],
        [*small_sends(), (gu_both, to_core), (down_slice, to_y)],
        lambda v: to_natural(v).astype(bf16),
        (block_out,),
    )
    small_sum = small_sum + small_got

    def core_whole(mine, other, axis):
        return swap(core, mine, other, axis).astype(f32)

    def gu_out(gu_both, gu_far, start):
        def of(value):
            return jnp.concatenate(
                [value[:, (2 * t + start) * tile : (2 * t + start + 1) * tile] for t in range(tiles)], 1
            )

        own = swap(ybit, of(gu_both[0]), of(gu_both[1]), 1)
        far = swap(ybit, of(gu_far[0]), of(gu_far[1]), 1)
        return core_whole(own, far, 1)

    down_total = high_reps(add(down_slice, down_got))
    small_got, (gate_grad, up_grad) = both_rounds(
        [in_s],
        small_sends(),
        lambda gu_both, gu_far: (gu_out(gu_both, gu_far, 0), gu_out(gu_both, gu_far, 1)),
        (gu_both, gu_far),
    )
    small_sum = small_added(small_got)
    finish(in_s)
    while len(small_moves) > 1:
        small_got, _ = ordered_round(small_sends())
        small_sum = small_added(small_got)
    in_slice = y_ordered(in_s.result(), 1)
    (down_away, in_got, *small_got), _ = ordered_round(
        [(down_total, to_core), (in_slice, to_y), *small_sends()]
    )
    small_sum = high_reps(small_added(small_got))
    in_total = high_reps(add(in_slice, in_got))
    (in_away,), down_grad = ordered_round(
        [(in_total, to_core)],
        lambda mine, other: down_in_order(core, mine, other),
        (down_total, down_away),
    )
    in_grad, out_grad = in_order(core, in_total, in_away, dq)
    small_total = lax.dynamic_slice_in_dim(
        small_sum, lax.axis_index("shard") * block, block, 1
    )
    return (
        block_natural,
        tokens_natural,
        small_total[0],
        in_grad,
        small_total[2:],
        out_grad,
        small_total[1],
        gate_grad,
        up_grad,
        down_grad,
    )


def solution(mesh):
    in_specs = (
        P(("rep", "shard"), None),
        P("shard"),
        P("shard", None),
        P(None, "shard"),
        P(None, "shard"),
        P("shard"),
        P("shard", None),
        P("shard", None),
        P(None, "shard"),
        P(("rep", "shard"), None),
    )
    out_specs = (
        P(("rep", "shard"), None),
        P(("rep", "shard"), None),
        P("shard"),
        P("shard", None),
        P(None, "shard"),
        P(None, "shard"),
        P("shard"),
        P("shard", None),
        P("shard", None),
        P(None, "shard"),
    )
    body = functools.partial(shards, mesh.shape["rep"], mesh.shape["shard"])
    return jax.shard_map(body, mesh=mesh, in_specs=in_specs, out_specs=out_specs, check_vma=False)
```
